512 devices in a mesh: ctx: 64 (over z, y_lo, core), head: 8 (over y_hi, x).
Axes of the slice: x: 4, y: 4 (y_hi: 2, y_lo: 2; y = y_hi * 2 + y_lo), z: 16, core: 2. Of those that a mesh axis runs over, the one named last changes fastest.
Arguments:
- span_states: bfloat16 [256, 64, 16384], P('ctx', None, 'head'), may hold values from -6 to 6
- kv_weight: bfloat16 [16384, 2048], P('ctx', 'head'), may hold values from -0.046875 to 0.046875
- q_weight: bfloat16 [16384, 16384], P('ctx', 'head'), may hold values from -0.046875 to 0.046875
- q_scale: float32 [16384], P('head'), may hold values from 0.1 to 1.9
- out_weight: bfloat16 [16384, 16384], P('head', 'ctx'), may hold values from -0.046875 to 0.046875
- decode_states: bfloat16 [2, 64, 16384], P(None, None, 'ctx'), may hold values from -6 to 6
- prior_keys: bfloat16 [64, 256, 1024], P('ctx', None, 'head'), may hold values from -128 to 128
- prior_values: bfloat16 [64, 256, 1024], P('ctx', None, 'head'), may hold values from -6 to 6
- key_scale: float32 [1024], P('head'), may hold values from 0.5 to 2
- cached_len: int32 [64], P('ctx'), may hold values from 1 to 256, as said below
Outputs:
- attn_out: bfloat16 [2, 64, 16384], P(None, 'head', 'ctx')
- new_keys: bfloat16 [64, 256, 1024], P('ctx', None, 'head')
- new_values: bfloat16 [64, 256, 1024], P('ctx', None, 'head')
The draws below stay inside these ranges and needn't reach their ends.
Inputs may be any that keep to these rules, and one draw needn't show every extreme that they name: `cached_len`: each sequence's cached length; some sequence has the full 256.
All inputs are finite; a program needn't handle non-finite values.
Results may differ from the reference program's by a relative error of at most 0.012.
The reference program's roundings to bfloat16 on the way count: a program that leaves them out, or rounds other values in their place, can miss the bound.
Values may be sent and summed in bfloat16 or wider, within the bound.
A program may use at most 64 MiB of HBM per device.

```python
import math
import jax
import jax.numpy as jnp
from jax import lax

D = 16384
HD = 128
GROUP = 16
KVH = 8
PRIOR = 256
STEPS = 2
SEQS = 64
SPAN = 256


def draw_prior_keys(key, part):
    key = jax.random.fold_in(key, 11)
    shape = (SEQS, PRIOR, KVH * HD)
    base = jax.random.normal(key, shape, jnp.float32)
    return base.astype(jnp.bfloat16)


def draw_cached_len(key, part):
    key = jax.random.fold_in(key, 23)
    first, second = jax.random.split(key)
    lengths = jax.random.randint(first, (SEQS,), 1, PRIOR + 1)
    chosen = jax.random.randint(second, (), 0, SEQS)
    return jnp.where(jnp.arange(SEQS) == chosen, PRIOR, lengths).astype(jnp.int32)


def block_scale(rng, shape, cuts, least, largest):
    loudness, own = 1.0, jax.random.fold_in(rng, 6)
    for dim, shards_of in cuts:
        steps = jnp.exp(jax.random.uniform(jax.random.fold_in(own, dim), (shards_of,), jnp.float32, least / len(cuts), largest / len(cuts)))
        loudness = loudness * jnp.repeat(steps, shape[dim] // shards_of).reshape([-1 if axis == dim else 1 for axis in range(len(shape))])
    return loudness


def gaussian(key, shape, spread, most, cuts=(), kind=jnp.bfloat16):
    factor_of = block_scale(key, shape, cuts, -0.22, 0.18) if cuts else 1.0
    array = jax.random.normal(key, shape, jnp.float32) * spread * factor_of
    return jnp.minimum(jnp.maximum(array, -most), most).astype(kind)


def setup_inputs(seed: int = 0) -> dict:
    arg_keys = jax.random.split(jax.random.key(seed), 11)
    span_states = gaussian(arg_keys[0], (SPAN, SEQS, D), 1.0, 6.0, ((0, 64), (2, 8)))
    kv_weight = gaussian(arg_keys[1], (D, KVH * 2 * HD), D ** -0.5, 0.046875, ((0, 64), (1, 8)))
    q_weight = gaussian(arg_keys[2], (D, KVH * GROUP * HD), D ** -0.5, 0.046875, ((0, 64), (1, 8)))
    q_scale = jnp.clip(1.0 + 0.18 * jax.random.normal(arg_keys[3], (KVH * GROUP * HD,), jnp.float32), 0.1, 1.9)
    out_weight = gaussian(arg_keys[4], (KVH * GROUP * HD, D), (KVH * GROUP * HD) ** -0.5, 0.046875, ((0, 8), (1, 64)))
    decode_states = gaussian(arg_keys[5], (STEPS, SEQS, D), 1.0, 6.0, ((2, 64),))
    prior_keys = draw_prior_keys(jax.random.fold_in(arg_keys[10], 71), 0)
    prior_values = gaussian(arg_keys[7], (SEQS, PRIOR, KVH * HD), 1.0, 6.0, ((0, 64), (2, 8)))
    key_scale = jnp.clip(jnp.exp(math.log(2.0) - 1.3862944 * jax.random.uniform(arg_keys[8], (KVH * HD,), jnp.float32) ** block_scale(arg_keys[8], (KVH * HD,), ((0, 8),), -0.2, 0.2)), 0.5, 2.0)
    cached_len = draw_cached_len(jax.random.fold_in(arg_keys[10], 71), 0)
    return {"span_states": span_states, "kv_weight": kv_weight, "q_weight": q_weight, "q_scale": q_scale, "out_weight": out_weight, "decode_states": decode_states, "prior_keys": prior_keys, "prior_values": prior_values, "key_scale": key_scale, "cached_len": cached_len}


def attend(queries, keys, values, valid):
    scores = jnp.einsum("sgd,skd->sgk", queries.astype(jnp.float32), keys.astype(jnp.float32))
    scores = jnp.where(valid[:, None, :], scores, jnp.float32(-1e30))
    top = jnp.max(scores, axis=-1, keepdims=True)
    weights = jnp.exp(scores - top)
    total = jnp.sum(weights, axis=-1, keepdims=True)
    rounded = weights.astype(jnp.bfloat16).astype(jnp.float32)
    mixed = jnp.einsum("sgk,skd->sgd", rounded, values.astype(jnp.float32)) / total
    return mixed.astype(jnp.bfloat16)


def reference(span_states, kv_weight, q_weight, q_scale, out_weight, decode_states, prior_keys, prior_values, key_scale, cached_len):
    scale_rows = key_scale.reshape(KVH, HD)
    block_kv = jnp.dot(span_states.reshape(SPAN * SEQS, D), kv_weight, preferred_element_type=jnp.float32)
    block_kv = block_kv.reshape(SPAN, SEQS, KVH, 2, HD)
    span_keys = (block_kv[:, :, :, 0, :] / scale_rows).astype(jnp.bfloat16).transpose(1, 0, 2, 3)
    span_values = block_kv[:, :, :, 1, :].astype(jnp.bfloat16).transpose(1, 0, 2, 3)
    new_keys = span_keys.reshape(SEQS, SPAN, KVH * HD)
    new_values = span_values.reshape(SEQS, SPAN, KVH * HD)
    prior_k = prior_keys.reshape(SEQS, PRIOR, KVH, HD).transpose(2, 0, 1, 3)
    prior_v = prior_values.reshape(SEQS, PRIOR, KVH, HD).transpose(2, 0, 1, 3)
    span_k = span_keys.transpose(2, 0, 1, 3)
    span_v = span_values.transpose(2, 0, 1, 3)
    valid_prior = jnp.arange(PRIOR, dtype=jnp.int32)[None, :] < cached_len[:, None]
    step_keys = []
    step_values = []
    outputs = []
    for step_index in range(STEPS):
        states = decode_states[step_index]
        query = jnp.dot(states, q_weight, preferred_element_type=jnp.float32) * q_scale
        fresh = jnp.dot(states, kv_weight, preferred_element_type=jnp.float32).reshape(SEQS, KVH, 2, HD)
        step_keys.append((fresh[:, :, 0, :] / scale_rows).astype(jnp.bfloat16))
        step_values.append(fresh[:, :, 1, :].astype(jnp.bfloat16))
        scaled = query.reshape(SEQS, KVH, GROUP, HD) * scale_rows[None, :, None, :] * (HD ** -0.5)
        scaled = scaled.astype(jnp.bfloat16).transpose(1, 0, 2, 3)
        recent_k = jnp.stack(step_keys, 1).transpose(2, 0, 1, 3)
        recent_v = jnp.stack(step_values, 1).transpose(2, 0, 1, 3)
        valid = jnp.concatenate([valid_prior, jnp.ones((SEQS, SPAN + step_index + 1), bool)], 1)

        def one_head(items):
            head_query, old_k, old_v, block_k, block_v, last_k, last_v = items
            keys = jnp.concatenate([old_k, block_k, last_k], 1)
            values = jnp.concatenate([old_v, block_v, last_v], 1)
            return attend(head_query, keys, values, valid)

        mixed = lax.map(one_head, (scaled, prior_k, prior_v, span_k, span_v, recent_k, recent_v))
        mixed = mixed.transpose(1, 0, 2, 3).reshape(SEQS, KVH * GROUP * HD)
        outputs.append(jnp.dot(mixed, out_weight, preferred_element_type=jnp.float32).astype(jnp.bfloat16))
    return jnp.stack(outputs), new_keys, new_values
```

```python
import functools

import jax
import jax.numpy as jnp
from jax import lax
from jax.experimental import pallas as pl
from jax.experimental.pallas import tpu as pltpu
from jax.sharding import PartitionSpec as P

MESH = pl.DeviceIdType.MESH
G = 4
F32 = jnp.float32
BF16 = jnp.bfloat16


def onehot(rows, cols, source):
    r = lax.broadcasted_iota(jnp.int32, (rows, cols), 0)
    k = lax.broadcasted_iota(jnp.int32, (rows, cols), 1)
    return jnp.where(k == source(r), 1.0, 0.0).astype(BF16)


def dot(a, b):
    return jnp.dot(a, b, preferred_element_type=F32)


def dot_t(a, b):
    return lax.dot_general(a, b, (((1,), (1,)), ((), ())), preferred_element_type=F32)


def kernel(
    nz, nh,
    span_ref, kvw_ref, qw_ref, qs_ref, ow_ref, dec_ref, pk_ref, pv_ref, ks_ref, cl_ref,
    out_ref, nk_ref, nv_ref,
    spanbuf, wbuf, part, rsbuf, a2abuf, kvnew,
    qbuf, qrecv1, qrecv2, qrow, qup, qdn, qsc, fk, fv,
    gath, gf, lhs, obuf, orecv,
    perm_s, w_r, up_s, dn_s,
    spc_s, spc_r, spy_s, spy_r, spf_s, spf_r,
    q1_s, q1_r, q2_s, q2_r, qu_s, qu_r, qd_s, qd_r,
    rs_s, rs_r, a2_s, a2_r, ga_s, ga_r, gy_s, gy_r, gc_s, gc_r, or_s, or_r,
):
    hpg = nh // G
    up_n, dn_n = nz // 2, nz // 2 - 1
    positions, seqs, feats = span_ref.shape
    hd = ks_ref.shape[1]
    group = qs_ref.shape[0]
    steps = dec_ref.shape[0] // seqs
    qcols = group * hd
    blk = positions * nz
    crows = kvw_ref.shape[0] // hpg
    c, h = lax.axis_index("ctx"), lax.axis_index("head")
    z, g = c // G, c % G
    yl, co = g // 2, g % 2
    core_dev = (z * G + yl * 2 + (1 - co), h)
    y_dev = (z * G + (1 - yl) * 2 + co, h)
    up_dev = (lax.rem(z + 1, nz) * G + g, h)
    dn_dev = (lax.rem(z + nz - 1, nz) * G + g, h)

    def zmod(a):
        return lax.rem(a + 2 * nz, nz)

    def rc(src, dst, ss, rs, dev):
        return pltpu.make_async_remote_copy(
            src_ref=src, dst_ref=dst, send_sem=ss, recv_sem=rs, device_id=dev, device_id_type=MESH
        )

    def other(dev):
        return jnp.logical_or(dev[0] != c, dev[1] != h)

    per = (G * nz) // nh

    def perm_to(r):
        zeta = lax.rem(c, per) * hpg + r
        return (zeta * G + h // hpg, c // per), zeta

    def perm_from(p):
        return (h * per + z // hpg, g * hpg + p)

    def rs_to(d):
        return (z * G + d % G, g * hpg + d // G)

    def rs_from(hs):
        return (z * G + h // hpg, hs)

    barrier = pltpu.get_barrier_semaphore()

    def greet(dev):
        pl.semaphore_signal(barrier, inc=1, device_id=dev, device_id_type=MESH)

    greet(core_dev)
    greet(y_dev)

    def greet_z(i, _):
        greet((zmod(z + i) * G + g, h))
        return 0

    def greet_h(i, _):
        greet((c, lax.rem(h + i, nh)))
        return 0

    lax.fori_loop(1, nz, greet_z, 0)
    lax.fori_loop(1, nh, greet_h, 0)
    for p in range(hpg):
        dev = perm_from(p)

        @pl.when(other(dev))
        def _():
            greet(dev)

    def greet_rs(hs, _):
        dev = rs_from(hs)

        @pl.when(other(dev))
        def _():
            greet(dev)

        return 0

    lax.fori_loop(0, nh, greet_rs, 0)

    order = onehot(seqs, seqs, lambda r: (r % nz) * G + r // nz)
    for p in range(positions):
        rows = dot(order, span_ref[p]).astype(BF16)
        for k in range(G):
            spanbuf[k, g, p * nz:(p + 1) * nz, :] = rows[k * nz:(k + 1) * nz]

    nrow = steps * seqs
    pick = onehot(
        nrow, nrow,
        lambda r: (r % steps) * seqs
        + ((r // steps) % nz) * G + ((r // (steps * nz)) % 2) * 2 + r // (steps * nz * 2),
    )
    decp = dot(pick, dec_ref[...]).astype(BF16)
    half = nrow // 2
    for k in range(2):
        qbuf[k, :, 0:qcols] = dot(decp[k * half:(k + 1) * half], qw_ref[...])
        qbuf[k, :, qcols:] = dot(decp[k * half:(k + 1) * half], kvw_ref[...])

    peers = 2 + (nz - 1) + (nh - 1)
    for r in range(hpg):
        peers = peers + jnp.where(other(perm_to(r)[0]), 1, 0)
    for d in range(nh):
        peers = peers + jnp.where(other(rs_to(d)), 1, 0)
    pl.semaphore_wait(barrier, peers)

    def wslot(p, zeta):
        return wbuf.at[p, pl.ds(pl.multiple_of(zeta * crows, crows), crows), :]

    def perm_copy(r):
        dev, zeta = perm_to(r)
        p = h % hpg
        return rc(kvw_ref.at[pl.ds(r * crows, crows), :], wslot(p, zeta), perm_s.at[r], w_r.at[p, zeta], dev), dev

    for r in range(hpg):
        copy, dev = perm_copy(r)

        @pl.when(other(dev))
        def _():
            copy.start()

        @pl.when(jnp.logical_not(other(dev)))
        def _():
            wslot(h % hpg, z)[...] = kvw_ref[r * crows:(r + 1) * crows, :]

    q1 = rc(qbuf.at[1 - co], qrecv1, q1_s, q1_r, core_dev)
    q1.start()
    spc = rc(spanbuf.at[:, g], spanbuf.at[:, g], spc_s, spc_r, core_dev)
    spc.start()
    q1.wait_recv()
    qh = half // 2
    for k in range(2):
        qbuf[co, k * qh:(k + 1) * qh, :] = qbuf[co, k * qh:(k + 1) * qh, :] + qrecv1[k * qh:(k + 1) * qh, :]
    q2 = rc(qbuf.at[co, pl.ds(pl.multiple_of((1 - yl) * qh, qh), qh), :], qrecv2, q2_s, q2_r, y_dev)
    q2.start()

    def spy(k):
        return rc(spanbuf.at[k, g], spanbuf.at[k, g], spy_s.at[k], spy_r.at[k], y_dev)

    def spf(k):
        gy = (1 - yl) * 2 + co
        return rc(spanbuf.at[k, gy], spanbuf.at[k, gy], spf_s.at[k], spf_r.at[k], core_dev)

    for k in range(G):
        spy(k).start()
    q2.wait_recv()
    own = qbuf[co, pl.ds(pl.multiple_of(yl * qh, qh), qh), :] + qrecv2[...]
    for r in range(qh):
        qrow[r, 0:1, :] = own[r:r + 1, :]

    def recv_w(p, zeta):
        rc(wslot(p, zeta), wslot(p, zeta), up_s.at[0, 0], w_r.at[p, zeta], up_dev).wait_recv()

    def send_up(s, p):
        zeta = zmod(z - s)
        return rc(wslot(p, zeta), wslot(p, zeta), up_s.at[s, p], w_r.at[p, zeta], up_dev)

    def send_dn(s, p):
        zeta = zmod(z + s)
        return rc(wslot(p, zeta), wslot(p, zeta), dn_s.at[s, p], w_r.at[p, zeta], dn_dev)

    def qpart(d):
        return qrow.at[pl.ds(d * steps, steps)]

    for p in range(hpg):
        dev = perm_from(p)

        @pl.when(other(dev))
        def _():
            recv_w(p, z)

        send_up(0, p).start()
        send_dn(0, p).start()

    def q_up(s):
        src = qpart(zmod(z + up_n)) if s == 0 else qup.at[s - 1]
        return rc(src, qup.at[s], qu_s.at[s], qu_r.at[s], up_dev)

    def q_dn(s):
        src = qpart(zmod(z - dn_n)) if s == 0 else qdn.at[s - 1]
        return rc(src, qdn.at[s], qd_s.at[s], qd_r.at[s], dn_dev)

    q_up(0).start()
    q_dn(0).start()
    for s in range(1, up_n):
        for p in range(hpg):
            recv_w(p, zmod(z - s))
            send_up(s, p).start()
            if s <= dn_n:
                recv_w(p, zmod(z + s))
            if s < dn_n:
                send_dn(s, p).start()
        q_up(s - 1).wait_recv()
        qup[s - 1] = qup[s - 1] + qpart(zmod(z + up_n - s))[...]
        q_up(s).start()
        if s < dn_n:
            q_dn(s - 1).wait_recv()
            qdn[s - 1] = qdn[s - 1] + qpart(zmod(z - dn_n + s))[...]
            q_dn(s).start()
        if s in (3, 5, 6):
            k = (3, 5, 6).index(s)
            spy(k).wait_recv()
            spf(k).start()
    for k in range(G):
        if k not in [(3, 5, 6).index(s) for s in range(1, up_n) if s in (3, 5, 6)]:
            spy(k).wait_recv()
            spf(k).start()
    for p in range(hpg):
        recv_w(p, zmod(z - up_n))
    spc.wait_recv()
    for k in range(G):
        spf(k).wait_recv()

    def rs_copy(d):
        return rc(part.at[d], rsbuf.at[h], rs_s.at[d], rs_r.at[h], rs_to(d))

    def product(i, _):
        d = lax.rem(i + h, nh)
        tile = spanbuf[d % G].reshape(G * blk, feats)
        part[d] = dot(tile, wbuf[d // G]).astype(BF16)
        away = other(rs_to(d))

        @pl.when(away)
        def _():
            rs_copy(d).start()

        @pl.when(jnp.logical_not(away))
        def _():
            rsbuf[h] = part[d]

        return 0

    lax.fori_loop(0, nh, product, 0)

    q_up(up_n - 1).wait_recv()
    q_dn(dn_n - 1).wait_recv()
    qv = qpart(z)[...] + qup[up_n - 1] + qdn[dn_n - 1]
    ks = ks_ref[...]
    fk[...] = jnp.zeros_like(fk)
    fv[...] = jnp.zeros_like(fv)
    for t in range(steps):
        for j in range(group):
            qsc[t * group + j:t * group + j + 1, :] = qv[t, 0:1, j * hd:(j + 1) * hd]
        fk[t:t + 1, :] = qv[t, 0:1, qcols:qcols + hd] / ks
        fv[t:t + 1, :] = qv[t, 0:1, qcols + hd:qcols + 2 * hd]
    scale = jnp.concatenate([qs_ref[...]] * steps, 0)
    scaled = (qsc[...] * scale * ks * (hd ** -0.5)).astype(BF16)
    s_old = dot_t(scaled, pk_ref[...])
    where = lax.broadcasted_iota(jnp.int32, s_old.shape, 1)
    s_old = jnp.where(where < cl_ref[0], s_old, -1e30)
    s_fresh = dot_t(scaled, fk[...].astype(BF16))
    col = lax.broadcasted_iota(jnp.int32, s_fresh.shape, 1)
    row = lax.broadcasted_iota(jnp.int32, s_fresh.shape, 0)
    s_fresh = jnp.where(col <= row // group, s_fresh, -1e30)
    top0 = jnp.maximum(jnp.max(s_old, 1, keepdims=True), jnp.max(s_fresh, 1, keepdims=True))

    for hs in range(nh):
        @pl.when(other(rs_from(hs)))
        def _():
            rc(rsbuf.at[hs], rsbuf.at[hs], rs_s.at[0], rs_r.at[hs], core_dev).wait_recv()

    total_kv = rsbuf[0].astype(F32)
    for hs in range(1, nh):
        total_kv = total_kv + rsbuf[hs].astype(F32)
    stored = jnp.concatenate([total_kv[:, :hd] / ks, total_kv[:, hd:]], 1).astype(BF16)
    pos = G * positions
    spread = onehot(G * blk, G * blk, lambda r: (r % pos) * nz + r // pos)
    a2abuf[...] = dot(spread, stored).astype(BF16).reshape(a2abuf.shape)

    def a2_copy(i):
        zt = zmod(z + i)
        return rc(a2abuf.at[zt], kvnew.at[z], a2_s.at[i], a2_r.at[z], (zt * G + g, h))

    def a2_start(i, _):
        a2_copy(i).start()
        return 0

    lax.fori_loop(1, nz, a2_start, 0)
    kvnew[z] = a2abuf[z]

    def a2_wait(i, _):
        zt = zmod(z + i)
        rc(kvnew.at[zt], kvnew.at[zt], a2_s.at[0], a2_r.at[zt], core_dev).wait_recv()
        return 0

    lax.fori_loop(1, nz, a2_wait, 0)
    kv = kvnew[...].reshape(nz * pos, 2 * hd)
    k_new, v_new = kv[:, :hd], kv[:, hd:]
    nk_ref[...] = k_new
    nv_ref[...] = v_new

    s_new = dot_t(scaled, k_new)
    top = jnp.maximum(top0, jnp.max(s_new, 1, keepdims=True))
    w_old, w_new, w_fresh = jnp.exp(s_old - top), jnp.exp(s_new - top), jnp.exp(s_fresh - top)
    total = (
        jnp.sum(w_old, 1, keepdims=True) + jnp.sum(w_new, 1, keepdims=True) + jnp.sum(w_fresh, 1, keepdims=True)
    )
    mixed = (
        dot(w_old.astype(BF16), pv_ref[...]) + dot(w_new.astype(BF16), v_new)
        + dot(w_fresh.astype(BF16), fv[...].astype(BF16))
    ) / total
    gath[z, g] = mixed.astype(BF16)

    def ga_copy(i):
        return rc(gath.at[z, g], gath.at[z, g], ga_s.at[i], ga_r.at[z], (zmod(z + i) * G + g, h))

    def ga_start(i, _):
        ga_copy(i).start()
        return 0

    lax.fori_loop(1, nz, ga_start, 0)

    def ga_wait(i, _):
        zt = zmod(z + i)
        rc(gath.at[zt, g], gath.at[zt, g], ga_s.at[0], ga_r.at[zt], core_dev).wait_recv()
        return 0

    lax.fori_loop(1, nz, ga_wait, 0)
    gy = rc(gath.at[:, g], gath.at[:, g], gy_s, gy_r, y_dev)
    gy.start()

    def gc_copy(k):
        gk = g if k == 0 else (1 - yl) * 2 + co
        return rc(gath.at[:, gk], gath.at[:, gk], gc_s.at[k], gc_r.at[k], core_dev)

    gc_copy(0).start()
    gy.wait_recv()
    gc_copy(1).start()
    gc_copy(0).wait_recv()
    gc_copy(1).wait_recv()

    gf[...] = gath[...].reshape(gf.shape).astype(F32)
    for t in range(steps):
        for j in range(group):
            rows = gf[pl.ds(t * group + j, seqs, stride=steps * group), :]
            lhs[t * seqs:(t + 1) * seqs, j * hd:(j + 1) * hd] = rows.astype(BF16)
    obuf[...] = dot(lhs[...], ow_ref[...]).reshape(obuf.shape)
    mine = seqs // nh

    def or_copy(i):
        ht = lax.rem(h + i, nh)
        src = obuf.at[:, pl.ds(pl.multiple_of(ht * mine, mine), mine), :]
        return rc(src, orecv.at[h], or_s.at[i], or_r.at[h], (c, ht))

    def or_start(i, _):
        or_copy(i).start()
        return 0

    lax.fori_loop(1, nh, or_start, 0)
    orecv[h] = obuf[:, pl.ds(pl.multiple_of(h * mine, mine), mine), :]

    def or_wait(i, _):
        hs = lax.rem(h + i, nh)
        rc(orecv.at[hs], orecv.at[hs], or_s.at[0], or_r.at[hs], core_dev).wait_recv()
        return 0

    lax.fori_loop(1, nh, or_wait, 0)
    result = orecv[0]
    for hs in range(1, nh):
        result = result + orecv[hs]
    out_ref[...] = result.astype(BF16)

    for r in range(hpg):
        copy, dev = perm_copy(r)

        @pl.when(other(dev))
        def _():
            copy.wait_send()

    q1.wait_send()
    q2.wait_send()
    spc.wait_send()
    for k in range(G):
        spy(k).wait_send()
        spf(k).wait_send()
    for s in range(up_n):
        for p in range(hpg):
            send_up(s, p).wait_send()
            if s < dn_n:
                send_dn(s, p).wait_send()
        q_up(s).wait_send()
        if s < dn_n:
            q_dn(s).wait_send()

    def rs_done(d, _):
        @pl.when(other(rs_to(d)))
        def _():
            rs_copy(d).wait_send()

        return 0

    lax.fori_loop(0, nh, rs_done, 0)

    def z_done(i, _):
        a2_copy(i).wait_send()
        ga_copy(i).wait_send()
        return 0

    lax.fori_loop(1, nz, z_done, 0)
    gy.wait_send()
    gc_copy(0).wait_send()
    gc_copy(1).wait_send()

    def or_done(i, _):
        or_copy(i).wait_send()
        return 0

    lax.fori_loop(1, nh, or_done, 0)


def body(
    span_states, kv_weight, q_weight, q_scale, out_weight, decode_states, prior_keys, prior_values, key_scale, cached_len
):
    nh = lax.axis_size("head")
    nz = lax.axis_size("ctx") // G
    hpg = nh // G
    positions, seqs, feats = span_states.shape
    hd = key_scale.shape[0]
    qcols = q_scale.shape[0]
    group = qcols // hd
    steps, _, depth = decode_states.shape
    width = qcols + 2 * hd
    nrow = steps * seqs
    blk = positions * nz
    pos = G * positions
    ocols = out_weight.shape[1]
    prior = prior_keys.shape[1]
    vm = pltpu.VMEM
    dma = pltpu.SemaphoreType.DMA
    up_n, dn_n = nz // 2, nz // 2 - 1
    vspec = pl.BlockSpec(memory_space=pltpu.VMEM)
    out, nk, nv = pl.pallas_call(
        functools.partial(kernel, nz, nh),
        out_shape=(
            jax.ShapeDtypeStruct((steps, seqs // nh, ocols), BF16),
            jax.ShapeDtypeStruct((nz * pos, hd), BF16),
            jax.ShapeDtypeStruct((nz * pos, hd), BF16),
        ),
        in_specs=[vspec] * 9 + [pl.BlockSpec(memory_space=pltpu.SMEM)],
        out_specs=(vspec,) * 3,
        scratch_shapes=[
            vm((G, G, blk, feats), BF16),
            vm((hpg, feats, 2 * hd), BF16),
            vm((nh, G * blk, 2 * hd), BF16),
            vm((nh, G * blk, 2 * hd), BF16),
            vm((nz, pos, 2 * hd), BF16),
            vm((nz, pos, 2 * hd), BF16),
            vm((2, nrow // 2, width), F32),
            vm((nrow // 2, width), F32),
            vm((nrow // 4, width), F32),
            vm((nrow // 4, 1, width), F32),
            vm((up_n, steps, 1, width), F32),
            vm((dn_n, steps, 1, width), F32),
            vm((steps * group, hd), F32),
            vm((16, hd), F32),
            vm((16, hd), F32),
            vm((nz, G, steps * group, hd), BF16),
            vm((seqs * steps * group, hd), F32),
            vm((nrow, qcols), BF16),
            vm((steps, seqs, ocols), F32),
            vm((nh, steps, seqs // nh, ocols), F32),
            dma((hpg,)), dma((hpg, nz)), dma((up_n, hpg)), dma((dn_n, hpg)),
            dma, dma, dma((G,)), dma((G,)), dma((G,)), dma((G,)),
            dma, dma, dma, dma, dma((up_n,)), dma((up_n,)), dma((dn_n,)), dma((dn_n,)),
            dma((nh,)), dma((nh,)), dma((nz,)), dma((nz,)), dma((nz,)), dma((nz,)),
            dma, dma, dma((2,)), dma((2,)), dma((nh,)), dma((nh,)),
        ],
        compiler_params=pltpu.CompilerParams(
            collective_id=0, has_side_effects=True, vmem_limit_bytes=40 * 2**20
        ),
        name="layer",
    )(
        span_states, kv_weight, q_weight, q_scale.reshape(group, hd), out_weight,
        decode_states.reshape(nrow, depth), prior_keys.reshape(prior, hd), prior_values.reshape(prior, hd),
        key_scale.reshape(1, hd), cached_len,
    )
    return out, nk.reshape(1, nz * pos, hd), nv.reshape(1, nz * pos, hd)


def solution(mesh):
    return jax.shard_map(
        body,
        mesh=mesh,
        in_specs=(
            P("ctx", None, "head"),
            P("ctx", "head"),
            P("ctx", "head"),
            P("head"),
            P("head", "ctx"),
            P(None, None, "ctx"),
            P("ctx", None, "head"),
            P("ctx", None, "head"),
            P("head"),
            P("ctx"),
        ),
        out_specs=(P(None, "head", "ctx"), P("ctx", None, "head"), P("ctx", None, "head")),
        check_vma=False,
    )
```

```python
import functools

import jax
import jax.numpy as jnp
from jax import lax
from jax.experimental import pallas as pl
from jax.experimental.pallas import tpu as pltpu
from jax.sharding import PartitionSpec as P

MESH = pl.DeviceIdType.MESH
G = 4
CUTS = 2
F32 = jnp.float32
BF16 = jnp.bfloat16


def onehot(rows, cols, source):
    r = lax.broadcasted_iota(jnp.int32, (rows, cols), 0)
    k = lax.broadcasted_iota(jnp.int32, (rows, cols), 1)
    return jnp.where(k == source(r), 1.0, 0.0).astype(BF16)


def dot(a, b):
    return jnp.dot(a, b, preferred_element_type=F32)


def dot_t(a, b):
    return lax.dot_general(a, b, (((1,), (1,)), ((), ())), preferred_element_type=F32)


def kernel(
    nz, nh,
    span_hbm, kvw_hbm, qw_hbm, qs_hbm, ow_hbm, dec_hbm, pk_hbm, pv_hbm, ks_hbm, cl_ref,
    out_ref, nk_ref, nv_ref,
    span_ref, kvw_ref, qw_ref, qs_ref, ow_ref, dec_ref, pk_ref, pv_ref, ks_ref, in_s,
    spanbuf, wbuf, part, rsbuf, a2abuf, kvnew,
    qbuf, qrecv1, qrecv2, qrow, qup, qdn, qsc, fk, fv,
    gath, gf, lhs, obuf, orecv,
    perm_s, perm_r, w_r, up_s, dn_s,
    spc_s, spc_r, spy_s, spy_r, spf_s, spf_r,
    q1_s, q1_r, q2_s, q2_r, qu_s, qu_r, qd_s, qd_r,
    rs_s, rs_r, a2_s, a2_r, ga_s, ga_r, gy_s, gy_r, gc_s, gc_r, or_s, or_r,
):
    hpg = nh // G
    up_n, dn_n = nz // 2, nz // 2 - 1
    positions, seqs, feats = span_ref.shape
    hd = ks_ref.shape[1]
    group = qs_ref.shape[0]
    steps = dec_ref.shape[0] // seqs
    qcols = group * hd
    blk = positions * nz
    crows = kvw_ref.shape[0] // hpg
    c, h = lax.axis_index("ctx"), lax.axis_index("head")
    z, g = c // G, c % G
    yl, co = g // 2, g % 2
    core_dev = (z * G + yl * 2 + (1 - co), h)
    y_dev = (z * G + (1 - yl) * 2 + co, h)
    up_dev = (lax.rem(z + 1, nz) * G + g, h)
    dn_dev = (lax.rem(z + nz - 1, nz) * G + g, h)

    def zmod(a):
        return lax.rem(a + 2 * nz, nz)

    def rc(src, dst, ss, rs, dev):
        return pltpu.make_async_remote_copy(
            src_ref=src, dst_ref=dst, send_sem=ss, recv_sem=rs, device_id=dev, device_id_type=MESH
        )

    def other(dev):
        return jnp.logical_or(dev[0] != c, dev[1] != h)

    per = (G * nz) // nh

    def perm_to(r):
        v = yl + 2 * co
        j = v if r == 0 else nz // 2 - 1 - v
        zeta = jnp.where(lax.rem(c, per) >= G, zmod(z + j), zmod(z - j))
        return (zeta * G + h // hpg, c // per)

    def slot_of(zeta):
        away = zmod(zeta - h * per // G)
        upper = jnp.logical_and(away >= 1, away <= nz // 2)
        j = jnp.where(upper, away - 1, lax.rem(nz - away, nz))
        r = jnp.where(j >= G, 1, 0)
        v = jnp.where(j >= G, nz // 2 - 1 - j, j)
        cl = jnp.where(upper, G, 0) + lax.rem(v, 2) * 2 + v // 2
        return cl, r

    def perm_from(p):
        cl, _ = slot_of(z)
        return (h * per + cl, g * hpg + p)

    def rs_to(d):
        return (z * G + d % G, g * hpg + d // G)

    def rs_from(hs):
        return (z * G + h // hpg, hs)

    pending = []

    def finish():
        for leave in pending:
            leave()

    def sent(*copies):
        pending.extend(copy.wait_send for copy in copies)

    fetches = [
        pltpu.make_async_copy(src, dst, in_s.at[i])
        for i, (src, dst) in enumerate((
            (dec_hbm, dec_ref), (qw_hbm, qw_ref), (kvw_hbm, kvw_ref), (span_hbm, span_ref), (ks_hbm, ks_ref),
            (qs_hbm, qs_ref), (pk_hbm, pk_ref), (pv_hbm, pv_ref), (ow_hbm, ow_ref),
        ))
    ]
    for fetch in fetches:
        fetch.start()

    barrier = pltpu.get_barrier_semaphore()

    def greet(dev):
        pl.semaphore_signal(barrier, inc=1, device_id=dev, device_id_type=MESH)

    greet(core_dev)
    greet(y_dev)

    def greet_z(i, _):
        greet((zmod(z + i) * G + g, h))
        return 0

    def greet_h(i, _):
        greet((c, lax.rem(h + i, nh)))
        return 0

    lax.fori_loop(1, nz, greet_z, 0)
    lax.fori_loop(1, nh, greet_h, 0)
    for p in range(hpg):
        dev = perm_from(p)

        @pl.when(other(dev))
        def _():
            greet(dev)

    def greet_rs(hs, _):
        dev = rs_from(hs)

        @pl.when(other(dev))
        def _():
            greet(dev)

        return 0

    lax.fori_loop(0, nh, greet_rs, 0)

    for i in range(4):
        fetches[i].wait()
    order = onehot(seqs, seqs, lambda r: (r % nz) * G + r // nz)
    for p in range(positions):
        rows = dot(order, span_ref[p]).astype(BF16)
        for k in range(G):
            spanbuf[k, g, p * nz:(p + 1) * nz, :] = rows[k * nz:(k + 1) * nz]

    nrow = steps * seqs
    pick = onehot(
        nrow, nrow,
        lambda r: (r % steps) * seqs
        + ((r // steps) % nz) * G + ((r // (steps * nz)) % 2) * 2 + r // (steps * nz * 2),
    )
    decp = dot(pick, dec_ref[...]).astype(BF16)
    half = nrow // 2
    for k in range(2):
        qbuf[k, :, 0:qcols] = dot(decp[k * half:(k + 1) * half], qw_ref[...])
        qbuf[k, :, qcols:] = dot(decp[k * half:(k + 1) * half], kvw_ref[...])

    peers = 2 + (nz - 1) + (nh - 1)
    for r in range(hpg):
        peers = peers + jnp.where(other(perm_to(r)), 1, 0)
    for d in range(nh):
        peers = peers + jnp.where(other(rs_to(d)), 1, 0)
    pl.semaphore_wait(barrier, peers)

    def wrows(p, slot):
        return wbuf.at[p, pl.ds(pl.multiple_of(slot * crows, crows), crows), :]

    prows = crows // CUTS

    def wslot(m, zeta):
        cl, r = slot_of(zeta)
        start = (cl * hpg + r) * crows + (m % CUTS) * prows
        return wbuf.at[m // CUTS, pl.ds(pl.multiple_of(start, prows), prows), :]

    def perm_copy(r):
        dev = perm_to(r)
        p = h % hpg
        slot = lax.rem(c, per) * hpg + r
        return rc(kvw_hbm.at[pl.ds(r * crows, crows), :], wrows(p, slot), perm_s.at[r], perm_r.at[p], dev), dev

    for r in range(hpg):
        copy, dev = perm_copy(r)

        @pl.when(other(dev))
        def _():
            copy.start()

        @pl.when(jnp.logical_not(other(dev)))
        def _():
            wrows(h % hpg, lax.rem(c, per) * hpg + r)[...] = kvw_ref[r * crows:(r + 1) * crows, :]

    for r in range(hpg):
        def leave(r=r):
            copy, dev = perm_copy(r)
            pl.when(other(dev))(copy.wait_send)

        pending.append(leave)

    q1 = rc(qbuf.at[1 - co], qrecv1, q1_s, q1_r, core_dev)
    q1.start()
    spc = rc(spanbuf.at[:, g], spanbuf.at[:, g], spc_s, spc_r, core_dev)
    spc.start()
    q1.wait_recv()
    qh = half // 2
    for k in range(2):
        qbuf[co, k * qh:(k + 1) * qh, :] = qbuf[co, k * qh:(k + 1) * qh, :] + qrecv1[k * qh:(k + 1) * qh, :]
    q2 = rc(qbuf.at[co, pl.ds(pl.multiple_of((1 - yl) * qh, qh), qh), :], qrecv2, q2_s, q2_r, y_dev)
    q2.start()

    def spy(k):
        return rc(spanbuf.at[k, g], spanbuf.at[k, g], spy_s.at[k], spy_r.at[k], y_dev)

    def spf(k):
        gy = (1 - yl) * 2 + co
        return rc(spanbuf.at[k, gy], spanbuf.at[k, gy], spf_s.at[k], spf_r.at[k], core_dev)

    for k in range(G):
        spy(k).start()
    sent(q1, q2, spc, *[spy(k) for k in range(G)])

    def recv_w(m, zeta):
        rc(wslot(m, zeta), wslot(m, zeta), up_s.at[0, 0], w_r.at[m, zeta], up_dev).wait_recv()

    def send_up(s, m):
        zeta = zmod(z - s)
        return rc(wslot(m, zeta), wslot(m, zeta), up_s.at[s, m], w_r.at[m, zeta], up_dev)

    def send_dn(s, m):
        zeta = zmod(z + s)
        return rc(wslot(m, zeta), wslot(m, zeta), dn_s.at[s, m], w_r.at[m, zeta], dn_dev)

    def qpart(d):
        return qrow.at[pl.ds(d * steps, steps)]

    for p in range(hpg):
        cl, r = slot_of(z)
        block = wrows(p, cl * hpg + r)
        pl.when(other(perm_from(p)))(rc(block, block, perm_s.at[0], perm_r.at[p], up_dev).wait_recv)
        for m in range(p * CUTS, (p + 1) * CUTS):
            send_up(0, m).start()
            send_dn(0, m).start()

    q2.wait_recv()
    own = qbuf[co, pl.ds(pl.multiple_of(yl * qh, qh), qh), :] + qrecv2[...]
    for r in range(qh):
        qrow[r, 0:1, :] = own[r:r + 1, :]

    def q_up(s):
        src = qpart(zmod(z + up_n)) if s == 0 else qup.at[s - 1]
        return rc(src, qup.at[s], qu_s.at[s], qu_r.at[s], up_dev)

    def q_dn(s):
        src = qpart(zmod(z - dn_n)) if s == 0 else qdn.at[s - 1]
        return rc(src, qdn.at[s], qd_s.at[s], qd_r.at[s], dn_dev)

    q_up(0).start()
    q_dn(0).start()
    parts = hpg * CUTS
    for s in range(1, up_n):
        for m in range(parts):
            recv_w(m, zmod(z - s))
            send_up(s, m).start()
            if s <= dn_n:
                recv_w(m, zmod(z + s))
            if s < dn_n:
                send_dn(s, m).start()
            if m == parts // 2 - 1:
                q_up(s - 1).wait_recv()
                qup[s - 1] = qup[s - 1] + qpart(zmod(z + up_n - s))[...]
                q_up(s).start()
                if s < dn_n:
                    q_dn(s - 1).wait_recv()
                    qdn[s - 1] = qdn[s - 1] + qpart(zmod(z - dn_n + s))[...]
                    q_dn(s).start()
        k = s - up_n + G
        if k >= 0:
            spy(k).wait_recv()
            spf(k).start()
    for m in range(parts):
        recv_w(m, zmod(z - up_n))
    spc.wait_recv()
    for k in range(G):
        spf(k).wait_recv()

    sent(*[spf(k) for k in range(G)])
    for s in range(up_n):
        sent(*[send_up(s, m) for m in range(parts)], q_up(s))
        if s < dn_n:
            sent(*[send_dn(s, m) for m in range(parts)], q_dn(s))

    def rs_copy(d, kind):
        return rc(part.at[d, kind], rsbuf.at[h, kind], rs_s.at[d, kind], rs_r.at[h, kind], rs_to(d))

    def product(i, _):
        d = lax.rem(i + h, nh)
        tile = spanbuf[d % G].reshape(G * blk, feats)
        sums = dot(tile, wbuf[d // G]).astype(BF16)
        part[d, 0] = sums[:, :hd]
        part[d, 1] = sums[:, hd:]
        away = other(rs_to(d))

        @pl.when(away)
        def _():
            rs_copy(d, 0).start()

        @pl.when(jnp.logical_not(away))
        def _():
            rsbuf[h] = part[d]

        return 0

    lax.fori_loop(0, nh, product, 0)

    def send_values(i, _):
        d = lax.rem(i + h, nh)
        pl.when(other(rs_to(d)))(lambda: rs_copy(d, 1).start())
        return 0

    lax.fori_loop(0, nh, send_values, 0)

    def rs_done(d, _):
        @pl.when(other(rs_to(d)))
        def _():
            rs_copy(d, 0).wait_send()
            rs_copy(d, 1).wait_send()

        return 0

    pending.append(lambda: lax.fori_loop(0, nh, rs_done, 0))

    q_up(up_n - 1).wait_recv()
    q_dn(dn_n - 1).wait_recv()
    qv = qpart(z)[...] + qup[up_n - 1] + qdn[dn_n - 1]
    for i in range(4, len(fetches)):
        fetches[i].wait()
    ks = ks_ref[...]
    fk[...] = jnp.zeros_like(fk)
    fv[...] = jnp.zeros_like(fv)
    for t in range(steps):
        for j in range(group):
            qsc[t * group + j:t * group + j + 1, :] = qv[t, 0:1, j * hd:(j + 1) * hd]
        fk[t:t + 1, :] = qv[t, 0:1, qcols:qcols + hd] / ks
        fv[t:t + 1, :] = qv[t, 0:1, qcols + hd:qcols + 2 * hd]
    scale = jnp.concatenate([qs_ref[...]] * steps, 0)
    scaled = (qsc[...] * scale * ks * (hd ** -0.5)).astype(BF16)
    s_old = dot_t(scaled, pk_ref[...])
    where = lax.broadcasted_iota(jnp.int32, s_old.shape, 1)
    s_old = jnp.where(where < cl_ref[0], s_old, -1e30)
    s_fresh = dot_t(scaled, fk[...].astype(BF16))
    col = lax.broadcasted_iota(jnp.int32, s_fresh.shape, 1)
    row = lax.broadcasted_iota(jnp.int32, s_fresh.shape, 0)
    s_fresh = jnp.where(col <= row // group, s_fresh, -1e30)
    top0 = jnp.maximum(jnp.max(s_old, 1, keepdims=True), jnp.max(s_fresh, 1, keepdims=True))

    pos = G * positions
    spread = onehot(G * blk, G * blk, lambda r: (r % pos) * nz + r // pos)

    def a2_copy(i, kind):
        zt = zmod(z + i)
        return rc(a2abuf.at[kind, zt], kvnew.at[kind, z], a2_s.at[kind, i], a2_r.at[kind, z], (zt * G + g, h))

    def a2_done(i, _):
        a2_copy(i, 0).wait_send()
        a2_copy(i, 1).wait_send()
        return 0

    for kind in range(2):
        for hs in range(nh):
            slot = rsbuf.at[hs, kind]
            pl.when(other(rs_from(hs)))(rc(slot, slot, rs_s.at[0, 0], rs_r.at[hs, kind], core_dev).wait_recv)
        sums = rsbuf[0, kind].astype(F32)
        for hs in range(1, nh):
            sums = sums + rsbuf[hs, kind].astype(F32)
        if kind == 0:
            sums = sums / ks
        a2abuf[kind] = dot(spread, sums.astype(BF16)).astype(BF16).reshape(nz, pos, hd)

        def a2_start(i, _, kind=kind):
            a2_copy(i, kind).start()
            return 0

        lax.fori_loop(1, nz, a2_start, 0)
        kvnew[kind, z] = a2abuf[kind, z]

    pending.append(lambda: lax.fori_loop(1, nz, a2_done, 0))

    def arrived(kind):
        def a2_wait(i, _):
            zt = zmod(z + i)
            slot = kvnew.at[kind, zt]
            rc(slot, slot, a2_s.at[0, 0], a2_r.at[kind, zt], core_dev).wait_recv()
            return 0

        lax.fori_loop(1, nz, a2_wait, 0)
        return kvnew[kind].reshape(nz * pos, hd)

    k_new = arrived(0)
    nk_ref[...] = k_new
    s_new = dot_t(scaled, k_new)
    top = jnp.maximum(top0, jnp.max(s_new, 1, keepdims=True))
    w_old, w_new, w_fresh = jnp.exp(s_old - top), jnp.exp(s_new - top), jnp.exp(s_fresh - top)
    total = (
        jnp.sum(w_old, 1, keepdims=True) + jnp.sum(w_new, 1, keepdims=True) + jnp.sum(w_fresh, 1, keepdims=True)
    )
    mixed = dot(w_old.astype(BF16), pv_ref[...]) + dot(w_fresh.astype(BF16), fv[...].astype(BF16))
    v_new = arrived(1)
    nv_ref[...] = v_new
    mixed = (mixed + dot(w_new.astype(BF16), v_new)) / total
    gath[z, g] = mixed.astype(BF16)

    gy_of = (1 - yl) * 2 + co

    def zig(i):
        return zmod(z + jnp.where(lax.rem(i, 2) == 1, (i + 1) // 2, -(i // 2)))

    def ga_copy(i):
        return rc(gath.at[z, g], gath.at[z, g], ga_s.at[i], ga_r.at[z], (zig(i) * G + g, h))

    def gy_copy(zt):
        return rc(gath.at[zt, g], gath.at[zt, g], gy_s.at[zt], gy_r.at[zt], y_dev)

    def gc_copy(zt, k):
        gk = g if k == 0 else gy_of
        return rc(gath.at[zt, gk], gath.at[zt, gk], gc_s.at[k, zt], gc_r.at[k, zt], core_dev)

    def ga_start(i, _):
        ga_copy(i).start()
        return 0

    lax.fori_loop(1, nz, ga_start, 0)
    gy_copy(z).start()
    gc_copy(z, 0).start()

    def hand_on(i, _):
        zt = zig(i)
        rc(gath.at[zt, g], gath.at[zt, g], ga_s.at[0], ga_r.at[zt], core_dev).wait_recv()
        gy_copy(zt).start()
        gc_copy(zt, 0).start()
        return 0

    def hand_over(i, _):
        zt = zig(i)
        rc(gath.at[zt, gy_of], gath.at[zt, gy_of], ga_s.at[0], gy_r.at[zt], core_dev).wait_recv()
        gc_copy(zt, 1).start()
        return 0

    def gc_wait(zt, _):
        for k in range(2):
            slot = gath.at[zt, (yl if k == 0 else 1 - yl) * 2 + 1 - co]
            rc(slot, slot, ga_s.at[0], gc_r.at[k, zt], core_dev).wait_recv()
        return 0

    lax.fori_loop(1, nz, hand_on, 0)
    lax.fori_loop(0, nz, hand_over, 0)
    lax.fori_loop(0, nz, gc_wait, 0)

    def ga_done(i, _):
        pl.when(i > 0)(lambda: ga_copy(i).wait_send())
        gy_copy(i).wait_send()
        gc_copy(i, 0).wait_send()
        gc_copy(i, 1).wait_send()
        return 0

    pending.append(lambda: lax.fori_loop(0, nz, ga_done, 0))

    gf[...] = gath[...].reshape(gf.shape).astype(F32)
    for t in range(steps):
        for j in range(group):
            rows = gf[pl.ds(t * group + j, seqs, stride=steps * group), :]
            lhs[t * seqs:(t + 1) * seqs, j * hd:(j + 1) * hd] = rows.astype(BF16)
    obuf[...] = dot(lhs[...], ow_ref[...]).reshape(obuf.shape)
    mine = seqs // nh

    def or_copy(i):
        ht = lax.rem(h + i, nh)
        src = obuf.at[:, pl.ds(pl.multiple_of(ht * mine, mine), mine), :]
        return rc(src, orecv.at[h], or_s.at[i], or_r.at[h], (c, ht))

    def or_start(i, _):
        or_copy(i).start()
        return 0

    lax.fori_loop(1, nh, or_start, 0)
    orecv[h] = obuf[:, pl.ds(pl.multiple_of(h * mine, mine), mine), :]

    def or_wait(i, _):
        hs = lax.rem(h + i, nh)
        rc(orecv.at[hs], orecv.at[hs], or_s.at[0], or_r.at[hs], core_dev).wait_recv()
        return 0

    lax.fori_loop(1, nh, or_wait, 0)
    def or_done(i, _):
        or_copy(i).wait_send()
        return 0

    pending.append(lambda: lax.fori_loop(1, nh, or_done, 0))
    result = orecv[0]
    for hs in range(1, nh):
        result = result + orecv[hs]
    out_ref[...] = result.astype(BF16)

    finish()


def body(
    span_states, kv_weight, q_weight, q_scale, out_weight, decode_states, prior_keys, prior_values, key_scale, cached_len
):
    nh = lax.axis_size("head")
    nz = lax.axis_size("ctx") // G
    hpg = nh // G
    positions, seqs, feats = span_states.shape
    hd = key_scale.shape[0]
    qcols = q_scale.shape[0]
    group = qcols // hd
    steps, _, depth = decode_states.shape
    width = qcols + 2 * hd
    nrow = steps * seqs
    blk = positions * nz
    pos = G * positions
    ocols = out_weight.shape[1]
    prior = prior_keys.shape[1]
    vm = pltpu.VMEM
    dma = pltpu.SemaphoreType.DMA
    up_n, dn_n = nz // 2, nz // 2 - 1
    vspec = pl.BlockSpec(memory_space=pltpu.VMEM)
    operands = (
        span_states, kv_weight, q_weight, q_scale.reshape(group, hd), out_weight,
        decode_states.reshape(nrow, depth), prior_keys.reshape(prior, hd), prior_values.reshape(prior, hd),
        key_scale.reshape(1, hd),
    )
    out, nk, nv = pl.pallas_call(
        functools.partial(kernel, nz, nh),
        out_shape=(
            jax.ShapeDtypeStruct((steps, seqs // nh, ocols), BF16),
            jax.ShapeDtypeStruct((nz * pos, hd), BF16),
            jax.ShapeDtypeStruct((nz * pos, hd), BF16),
        ),
        in_specs=[pl.BlockSpec(memory_space=pl.ANY)] * 9 + [pl.BlockSpec(memory_space=pltpu.SMEM)],
        out_specs=(vspec,) * 3,
        scratch_shapes=[
            *[vm(a.shape, a.dtype) for a in operands], dma((len(operands),)),
            vm((G, G, blk, feats), BF16),
            vm((hpg, feats, 2 * hd), BF16),
            vm((nh, 2, G * blk, hd), BF16),
            vm((nh, 2, G * blk, hd), BF16),
            vm((2, nz, pos, hd), BF16),
            vm((2, nz, pos, hd), BF16),
            vm((2, nrow // 2, width), F32),
            vm((nrow // 2, width), F32),
            vm((nrow // 4, width), F32),
            vm((nrow // 4, 1, width), F32),
            vm((up_n, steps, 1, width), F32),
            vm((dn_n, steps, 1, width), F32),
            vm((steps * group, hd), F32),
            vm((16, hd), F32),
            vm((16, hd), F32),
            vm((nz, G, steps * group, hd), BF16),
            vm((seqs * steps * group, hd), F32),
            vm((nrow, qcols), BF16),
            vm((steps, seqs, ocols), F32),
            vm((nh, steps, seqs // nh, ocols), F32),
            dma((hpg,)), dma((hpg,)), dma((hpg * CUTS, nz)), dma((up_n, hpg * CUTS)), dma((dn_n, hpg * CUTS)),
            dma, dma, dma((G,)), dma((G,)), dma((G,)), dma((G,)),
            dma, dma, dma, dma, dma((up_n,)), dma((up_n,)), dma((dn_n,)), dma((dn_n,)),
            dma((nh, 2)), dma((nh, 2)), dma((2, nz)), dma((2, nz)), dma((nz,)), dma((nz,)),
            dma((nz,)), dma((nz,)), dma((2, nz)), dma((2, nz)), dma((nh,)), dma((nh,)),
        ],
        compiler_params=pltpu.CompilerParams(
            collective_id=0, has_side_effects=True, vmem_limit_bytes=60 * 2**20
        ),
        name="layer",
    )(*operands, cached_len)
    return out, nk.reshape(1, nz * pos, hd), nv.reshape(1, nz * pos, hd)


def solution(mesh):
    return jax.shard_map(
        body,
        mesh=mesh,
        in_specs=(
            P("ctx", None, "head"),
            P("ctx", "head"),
            P("ctx", "head"),
            P("head"),
            P("head", "ctx"),
            P(None, None, "ctx"),
            P("ctx", None, "head"),
            P("ctx", None, "head"),
            P("head"),
            P("ctx"),
        ),
        out_specs=(P(None, "head", "ctx"), P("ctx", None, "head"), P("ctx", None, "head")),
        check_vma=False,
    )
```

```python
import functools

import jax
import jax.numpy as jnp
from jax import lax
from jax.experimental import pallas as pl
from jax.experimental.pallas import tpu as pltpu
from jax.sharding import PartitionSpec as P

MESH = pl.DeviceIdType.MESH
G = 4
CUTS = 2
F32 = jnp.float32
BF16 = jnp.bfloat16


def onehot(rows, cols, source):
    r = lax.broadcasted_iota(jnp.int32, (rows, cols), 0)
    k = lax.broadcasted_iota(jnp.int32, (rows, cols), 1)
    return jnp.where(k == source(r), 1.0, 0.0).astype(BF16)


def dot(a, b):
    return jnp.dot(a, b, preferred_element_type=F32)


def dot_t(a, b):
    return lax.dot_general(a, b, (((1,), (1,)), ((), ())), preferred_element_type=F32)


def kernel(
    nz, nh,
    span_hbm, kvw_hbm, qw_hbm, qs_hbm, ow_hbm, dec_hbm, pk_hbm, pv_hbm, ks_hbm, cl_hbm,
    out_ref, kv_ref,
    span_ref, kvw_ref, qw_ref, qs_ref, ow_ref, dec_ref, pk_ref, pv_ref, ks_ref, cl_ref, in_s,
    spanbuf, wbuf, part, rsbuf, a2abuf, kvnew,
    qbuf, qrecv1, qrecv2, qrow, qup, qdn, qsc, fk, fv,
    gath, gf, lhs, obuf, orecv,
    perm_s, perm_r, w_r, up_s, dn_s,
    spc_s, spc_r, spy_s, spy_r, spf_s, spf_r,
    q1_s, q1_r, q2_s, q2_r, qu_s, qu_r, qd_s, qd_r,
    rs_s, rs_r, a2_s, a2_r, ga_s, ga_r, gy_s, gy_r, gc_s, gc_r, or_s, or_r,
):
    hpg = nh // G
    up_n, dn_n = nz // 2, nz // 2 - 1
    positions, seqs, feats = span_ref.shape
    hd = ks_ref.shape[1]
    group = qs_ref.shape[0]
    steps = dec_ref.shape[0] // seqs
    qcols = group * hd
    blk = positions * nz
    crows = kvw_ref.shape[0] // hpg
    c, h = lax.axis_index("ctx"), lax.axis_index("head")
    z, g = c // G, c % G
    yl, co = g // 2, g % 2
    core_dev = (z * G + yl * 2 + (1 - co), h)
    y_dev = (z * G + (1 - yl) * 2 + co, h)
    up_dev = (lax.rem(z + 1, nz) * G + g, h)
    dn_dev = (lax.rem(z + nz - 1, nz) * G + g, h)

    def zmod(a):
        return lax.rem(a + 2 * nz, nz)

    def rc(src, dst, ss, rs, dev):
        return pltpu.make_async_remote_copy(
            src_ref=src, dst_ref=dst, send_sem=ss, recv_sem=rs, device_id=dev, device_id_type=MESH
        )

    def other(dev):
        return jnp.logical_or(dev[0] != c, dev[1] != h)

    def group_of(head):
        pair = head // hpg
        return (pair // 2 + pair % 2) % 2 * 2 + pair % 2

    def heads_of(p):
        return ((co + yl) % 2 * 2 + co) * hpg + p

    per = (G * nz) // nh

    def perm_to(r):
        v = yl + 2 * co
        j = v if r == 0 else nz // 2 - 1 - v
        zeta = jnp.where(lax.rem(c, per) >= G, zmod(z + j), zmod(z - j))
        return (zeta * G + group_of(h), c // per)

    def slot_of(zeta):
        away = zmod(zeta - h * per // G)
        upper = jnp.logical_and(away >= 1, away <= nz // 2)
        j = jnp.where(upper, away - 1, lax.rem(nz - away, nz))
        r = jnp.where(j >= G, 1, 0)
        v = jnp.where(j >= G, nz // 2 - 1 - j, j)
        cl = jnp.where(upper, G, 0) + lax.rem(v, 2) * 2 + v // 2
        return cl, r

    def perm_from(p):
        cl, _ = slot_of(z)
        return (h * per + cl, heads_of(p))

    def rs_to(d):
        return (z * G + d % G, heads_of(d // G))

    def rs_from(hs):
        return (z * G + group_of(h), hs)

    pending = []

    def finish():
        for leave in pending:
            leave()

    def sent(*copies):
        pending.extend(copy.wait_send for copy in copies)

    fetches = [
        pltpu.make_async_copy(src, dst, in_s.at[i])
        for i, (src, dst) in enumerate((
            (dec_hbm, dec_ref), (qw_hbm, qw_ref), (kvw_hbm, kvw_ref), (span_hbm, span_ref), (ks_hbm, ks_ref),
            (qs_hbm, qs_ref), (pk_hbm, pk_ref), (pv_hbm, pv_ref), (ow_hbm, ow_ref), (cl_hbm, cl_ref),
        ))
    ]
    for fetch in fetches:
        fetch.start()

    barrier = pltpu.get_barrier_semaphore()

    def greet(dev):
        pl.semaphore_signal(barrier, inc=1, device_id=dev, device_id_type=MESH)

    greet(core_dev)
    greet(y_dev)

    def greet_z(i, _):
        greet((zmod(z + i) * G + g, h))
        return 0

    def greet_h(i, _):
        greet((c, lax.rem(h + i, nh)))
        return 0

    lax.fori_loop(1, nz, greet_z, 0)
    lax.fori_loop(1, nh, greet_h, 0)
    for p in range(hpg):
        dev = perm_from(p)

        @pl.when(other(dev))
        def _():
            greet(dev)

    def greet_rs(hs, _):
        dev = rs_from(hs)

        @pl.when(other(dev))
        def _():
            greet(dev)

        return 0

    lax.fori_loop(0, nh, greet_rs, 0)

    peers = 2 + (nz - 1) + (nh - 1)
    for r in range(hpg):
        peers = peers + jnp.where(other(perm_to(r)), 1, 0)
    for d in range(nh):
        peers = peers + jnp.where(other(rs_to(d)), 1, 0)
    pl.semaphore_wait(barrier, peers)

    def wrows(p, slot):
        return wbuf.at[p, pl.ds(pl.multiple_of(slot * crows, crows), crows), :]

    prows = crows // CUTS

    def wslot(m, zeta):
        cl, r = slot_of(zeta)
        start = (cl * hpg + r) * crows + (m % CUTS) * prows
        return wbuf.at[m // CUTS, pl.ds(pl.multiple_of(start, prows), prows), :]

    def perm_copy(r):
        dev = perm_to(r)
        p = h % hpg
        slot = lax.rem(c, per) * hpg + r
        return rc(kvw_hbm.at[pl.ds(r * crows, crows), :], wrows(p, slot), perm_s.at[r], perm_r.at[p], dev), dev

    for r in range(hpg):
        copy, dev = perm_copy(r)

        @pl.when(other(dev))
        def _():
            copy.start()

        @pl.when(jnp.logical_not(other(dev)))
        def _():
            here = wrows(h % hpg, lax.rem(c, per) * hpg + r)
            own_block = pltpu.make_async_copy(kvw_hbm.at[pl.ds(r * crows, crows), :], here, perm_s.at[r])
            own_block.start()
            own_block.wait()

    for r in range(hpg):
        def leave(r=r):
            copy, dev = perm_copy(r)
            pl.when(other(dev))(copy.wait_send)

        pending.append(leave)

    for i in range(4):
        fetches[i].wait()
    order = onehot(seqs, seqs, lambda r: (r % nz) * G + r // nz)
    for p in range(positions):
        rows = dot(order, span_ref[p]).astype(BF16)
        for k in range(G):
            spanbuf[k, g, p * nz:(p + 1) * nz, :] = rows[k * nz:(k + 1) * nz]

    nrow = steps * seqs
    pick = onehot(
        nrow, nrow,
        lambda r: (r % steps) * seqs
        + ((r // steps) % nz) * G + ((r // (steps * nz)) % 2) * 2 + r // (steps * nz * 2),
    )
    decp = dot(pick, dec_ref[...]).astype(BF16)
    half = nrow // 2
    for k in range(2):
        qbuf[k, :, 0:qcols] = dot(decp[k * half:(k + 1) * half], qw_ref[...])
        qbuf[k, :, qcols:] = dot(decp[k * half:(k + 1) * half], kvw_ref[...])

    q1 = rc(qbuf.at[1 - co], qrecv1, q1_s, q1_r, core_dev)
    q1.start()
    spc = rc(spanbuf.at[:, g], spanbuf.at[:, g], spc_s, spc_r, core_dev)
    spc.start()
    q1.wait_recv()
    qh = half // 2
    for k in range(2):
        qbuf[co, k * qh:(k + 1) * qh, :] = qbuf[co, k * qh:(k + 1) * qh, :] + qrecv1[k * qh:(k + 1) * qh, :]
    q2 = rc(qbuf.at[co, pl.ds(pl.multiple_of((1 - yl) * qh, qh), qh), :], qrecv2, q2_s, q2_r, y_dev)
    q2.start()

    def spy(k):
        return rc(spanbuf.at[k, g], spanbuf.at[k, g], spy_s.at[k], spy_r.at[k], y_dev)

    def spf(k):
        gy = (1 - yl) * 2 + co
        return rc(spanbuf.at[k, gy], spanbuf.at[k, gy], spf_s.at[k], spf_r.at[k], core_dev)

    for k in range(G):
        spy(k).start()
    sent(q1, q2, spc, *[spy(k) for k in range(G)])

    def recv_w(m, zeta):
        rc(wslot(m, zeta), wslot(m, zeta), up_s.at[0, 0], w_r.at[m, zeta], up_dev).wait_recv()

    def send_up(s, m):
        zeta = zmod(z - s)
        return rc(wslot(m, zeta), wslot(m, zeta), up_s.at[s, m], w_r.at[m, zeta], up_dev)

    def send_dn(s, m):
        zeta = zmod(z + s)
        return rc(wslot(m, zeta), wslot(m, zeta), dn_s.at[s, m], w_r.at[m, zeta], dn_dev)

    def qpart(d):
        return qrow.at[pl.ds(d * steps, steps)]

    for p in range(hpg):
        cl, r = slot_of(z)
        block = wrows(p, cl * hpg + r)
        pl.when(other(perm_from(p)))(rc(block, block, perm_s.at[0], perm_r.at[p], up_dev).wait_recv)
        for m in range(p * CUTS, (p + 1) * CUTS):
            send_up(0, m).start()
            send_dn(0, m).start()

    def q_up(s):
        src = qpart(zmod(z + up_n)) if s == 0 else qup.at[s - 1]
        return rc(src, qup.at[s], qu_s.at[s], qu_r.at[s], up_dev)

    def q_dn(s):
        src = qpart(zmod(z - dn_n)) if s == 0 else qdn.at[s - 1]
        return rc(src, qdn.at[s], qd_s.at[s], qd_r.at[s], dn_dev)

    def q_step(s):
        if s == 0:
            q2.wait_recv()
            own = qbuf[co, pl.ds(pl.multiple_of(yl * qh, qh), qh), :] + qrecv2[...]
            for r in range(qh):
                qrow[r, 0:1, :] = own[r:r + 1, :]
        else:
            q_up(s - 1).wait_recv()
            qup[s - 1] = qup[s - 1] + qpart(zmod(z + up_n - s))[...]
        q_up(s).start()
        if s < dn_n:
            if s > 0:
                q_dn(s - 1).wait_recv()
                qdn[s - 1] = qdn[s - 1] + qpart(zmod(z - dn_n + s))[...]
            q_dn(s).start()

    parts = hpg * CUTS

    def goes_up(s, m):
        return s < up_n - 1 or m < parts // 2

    def goes_dn(s, m):
        return s < up_n - 1 or m >= parts // 2

    for s in range(1, up_n):
        for m in range(parts):
            recv_w(m, zmod(z - s))
            if goes_up(s, m):
                send_up(s, m).start()
            recv_w(m, zmod(z + s))
            if goes_dn(s, m):
                send_dn(s, m).start()
            if m == parts // 2 - 1 and s >= 2:
                q_step(s - 2)
        k = s - up_n + G
        if k >= 0:
            spy(k).wait_recv()
            spf(k).start()
    q_step(up_n - 2)
    for m in range(parts):
        recv_w(m, zmod(z - up_n))
    spc.wait_recv()
    for k in range(G):
        spf(k).wait_recv()

    sent(*[spf(k) for k in range(G)])
    for s in range(up_n):
        sent(*[send_up(s, m) for m in range(parts) if goes_up(s, m)], q_up(s))
        sent(*[send_dn(s, m) for m in range(parts) if goes_dn(s, m)])
        if s < dn_n:
            sent(q_dn(s))

    def rs_copy(d, kind):
        return rc(part.at[d, kind], rsbuf.at[h, kind], rs_s.at[d, kind], rs_r.at[h, kind], rs_to(d))

    def product(i, _):
        d = lax.rem(i + h, nh)
        tile = spanbuf[d % G].reshape(G * blk, feats)
        sums = dot(tile, wbuf[d // G]).astype(BF16)
        part[d, 0] = sums[:, :hd]
        part[d, 1] = sums[:, hd:]
        away = other(rs_to(d))

        @pl.when(away)
        def _():
            rs_copy(d, 0).start()

        @pl.when(jnp.logical_not(away))
        def _():
            rsbuf[h] = part[d]

        return 0

    lax.fori_loop(0, nh, product, 0)

    def send_values(i, _):
        d = lax.rem(i + h, nh)
        pl.when(other(rs_to(d)))(lambda: rs_copy(d, 1).start())
        return 0

    lax.fori_loop(0, nh, send_values, 0)

    def rs_done(d, _):
        @pl.when(other(rs_to(d)))
        def _():
            rs_copy(d, 0).wait_send()
            rs_copy(d, 1).wait_send()

        return 0

    pending.append(lambda: lax.fori_loop(0, nh, rs_done, 0))

    q_step(up_n - 1)
    q_up(up_n - 1).wait_recv()
    q_dn(dn_n - 1).wait_recv()
    qv = qpart(z)[...] + qup[up_n - 1] + qdn[dn_n - 1]
    for i in range(4, len(fetches)):
        fetches[i].wait()
    ks = ks_ref[...]
    fk[...] = jnp.zeros_like(fk)
    fv[...] = jnp.zeros_like(fv)
    for t in range(steps):
        for j in range(group):
            qsc[t * group + j:t * group + j + 1, :] = qv[t, 0:1, j * hd:(j + 1) * hd]
        fk[t:t + 1, :] = qv[t, 0:1, qcols:qcols + hd] / ks
        fv[t:t + 1, :] = qv[t, 0:1, qcols + hd:qcols + 2 * hd]
    scale = jnp.concatenate([qs_ref[...]] * steps, 0)
    scaled = (qsc[...] * scale * ks * (hd ** -0.5)).astype(BF16)
    s_old = dot_t(scaled, pk_ref[...])
    where = lax.broadcasted_iota(jnp.int32, s_old.shape, 1)
    s_old = jnp.where(where < cl_ref[0], s_old, -1e30)
    s_fresh = dot_t(scaled, fk[...].astype(BF16))
    col = lax.broadcasted_iota(jnp.int32, s_fresh.shape, 1)
    row = lax.broadcasted_iota(jnp.int32, s_fresh.shape, 0)
    s_fresh = jnp.where(col <= row // group, s_fresh, -1e30)
    top0 = jnp.maximum(jnp.max(s_old, 1, keepdims=True), jnp.max(s_fresh, 1, keepdims=True))

    pos = G * positions
    spread = onehot(G * blk, G * blk, lambda r: (r % pos) * nz + r // pos)

    def zig(i):
        return zmod(z + jnp.where(lax.rem(i, 2) == 1, (i + 1) // 2, -(i // 2)))

    def a2_copy(i, kind):
        zt = zig(nz - i)
        return rc(a2abuf.at[kind, zt], kvnew.at[kind, z], a2_s.at[kind, i], a2_r.at[kind, z], (zt * G + g, h))

    def a2_done(i, _):
        a2_copy(i, 0).wait_send()
        a2_copy(i, 1).wait_send()
        return 0

    for kind in range(2):
        for hs in range(nh):
            slot = rsbuf.at[hs, kind]
            pl.when(other(rs_from(hs)))(rc(slot, slot, rs_s.at[0, 0], rs_r.at[hs, kind], core_dev).wait_recv)
        sums = rsbuf[0, kind].astype(F32)
        for hs in range(1, nh):
            sums = sums + rsbuf[hs, kind].astype(F32)
        if kind == 0:
            sums = sums / ks
        a2abuf[kind] = dot(spread, sums.astype(BF16)).astype(BF16).reshape(nz, pos, hd)

        def a2_start(i, _, kind=kind):
            a2_copy(i, kind).start()
            return 0

        lax.fori_loop(1, nz, a2_start, 0)
        kvnew[kind, z] = a2abuf[kind, z]

    pending.append(lambda: lax.fori_loop(1, nz, a2_done, 0))

    def arrived(kind):
        def a2_wait(i, _):
            zt = zig(i)
            slot = kvnew.at[kind, zt]
            rc(slot, slot, a2_s.at[0, 0], a2_r.at[kind, zt], core_dev).wait_recv()
            return 0

        lax.fori_loop(1, nz, a2_wait, 0)
        return kvnew[kind].reshape(nz * pos, hd)

    k_new = arrived(0)
    s_new = dot_t(scaled, k_new)
    top = jnp.maximum(top0, jnp.max(s_new, 1, keepdims=True))
    w_old, w_new, w_fresh = jnp.exp(s_old - top), jnp.exp(s_new - top), jnp.exp(s_fresh - top)
    total = (
        jnp.sum(w_old, 1, keepdims=True) + jnp.sum(w_new, 1, keepdims=True) + jnp.sum(w_fresh, 1, keepdims=True)
    )
    mixed = dot(w_old.astype(BF16), pv_ref[...]) + dot(w_fresh.astype(BF16), fv[...].astype(BF16))
    v_new = arrived(1)
    kv_ref[...] = kvnew[...].reshape(kv_ref.shape)
    mixed = (mixed + dot(w_new.astype(BF16), v_new)) / total
    gath[z, g] = mixed.astype(BF16)

    gy_of = (1 - yl) * 2 + co

    def ga_copy(i):
        return rc(gath.at[z, g], gath.at[z, g], ga_s.at[i], ga_r.at[z], (zig(nz - i) * G + g, h))

    def gy_copy(zt):
        return rc(gath.at[zt, g], gath.at[zt, g], gy_s.at[zt], gy_r.at[zt], y_dev)

    def gc_copy(zt, k):
        gk = g if k == 0 else gy_of
        return rc(gath.at[zt, gk], gath.at[zt, gk], gc_s.at[k, zt], gc_r.at[k, zt], core_dev)

    def ga_start(i, _):
        ga_copy(i).start()
        return 0

    lax.fori_loop(1, nz, ga_start, 0)
    gy_copy(z).start()
    gc_copy(z, 0).start()

    def hand_on(i, _):
        zt = zig(i)
        rc(gath.at[zt, g], gath.at[zt, g], ga_s.at[0], ga_r.at[zt], core_dev).wait_recv()
        gy_copy(zt).start()
        gc_copy(zt, 0).start()
        return 0

    def hand_over(i, _):
        zt = zig(i)
        rc(gath.at[zt, gy_of], gath.at[zt, gy_of], ga_s.at[0], gy_r.at[zt], core_dev).wait_recv()
        gc_copy(zt, 1).start()
        return 0

    def gc_wait(zt, _):
        for k in range(2):
            slot = gath.at[zt, (yl if k == 0 else 1 - yl) * 2 + 1 - co]
            rc(slot, slot, ga_s.at[0], gc_r.at[k, zt], core_dev).wait_recv()
        return 0

    lax.fori_loop(1, nz, hand_on, 0)
    lax.fori_loop(0, nz, hand_over, 0)
    lax.fori_loop(0, nz, gc_wait, 0)

    def ga_done(i, _):
        pl.when(i > 0)(lambda: ga_copy(i).wait_send())
        gy_copy(i).wait_send()
        gc_copy(i, 0).wait_send()
        gc_copy(i, 1).wait_send()
        return 0

    pending.append(lambda: lax.fori_loop(0, nz, ga_done, 0))

    gf[...] = gath[...].reshape(gf.shape).astype(F32)
    for t in range(steps):
        for j in range(group):
            rows = gf[pl.ds(t * group + j, seqs, stride=steps * group), :]
            lhs[t * seqs:(t + 1) * seqs, j * hd:(j + 1) * hd] = rows.astype(BF16)
    obuf[...] = dot(lhs[...], ow_ref[...]).reshape(obuf.shape)
    mine = seqs // nh

    def or_copy(i):
        ht = lax.rem(h + i, nh)
        src = obuf.at[:, pl.ds(pl.multiple_of(ht * mine, mine), mine), :]
        return rc(src, orecv.at[h], or_s.at[i], or_r.at[h], (c, ht))

    def or_start(i, _):
        or_copy(i).start()
        return 0

    lax.fori_loop(1, nh, or_start, 0)
    orecv[h] = obuf[:, pl.ds(pl.multiple_of(h * mine, mine), mine), :]

    def or_wait(i, _):
        hs = lax.rem(h + i, nh)
        rc(orecv.at[hs], orecv.at[hs], or_s.at[0], or_r.at[hs], core_dev).wait_recv()
        return 0

    lax.fori_loop(1, nh, or_wait, 0)
    def or_done(i, _):
        or_copy(i).wait_send()
        return 0

    pending.append(lambda: lax.fori_loop(1, nh, or_done, 0))
    result = orecv[0]
    for hs in range(1, nh):
        result = result + orecv[hs]
    out_ref[...] = result.astype(BF16)

    finish()


def place(out_ref, kv_ref, attn_ref, nk_ref, nv_ref, sems):
    moves = [
        pltpu.make_async_copy(src, dst, sems.at[i])
        for i, (src, dst) in enumerate(((kv_ref.at[0], nk_ref.at[0]), (kv_ref.at[1], nv_ref.at[0]), (out_ref, attn_ref)))
    ]
    for move in moves:
        move.start()
    for move in moves:
        move.wait()


def body(
    span_states, kv_weight, q_weight, q_scale, out_weight, decode_states, prior_keys, prior_values, key_scale, cached_len
):
    nh = lax.axis_size("head")
    nz = lax.axis_size("ctx") // G
    hpg = nh // G
    positions, seqs, feats = span_states.shape
    hd = key_scale.shape[0]
    qcols = q_scale.shape[0]
    group = qcols // hd
    steps, _, depth = decode_states.shape
    width = qcols + 2 * hd
    nrow = steps * seqs
    blk = positions * nz
    pos = G * positions
    ocols = out_weight.shape[1]
    prior = prior_keys.shape[1]
    vm = pltpu.VMEM
    dma = pltpu.SemaphoreType.DMA
    up_n, dn_n = nz // 2, nz // 2 - 1
    vspec = pl.BlockSpec(memory_space=pltpu.VMEM)
    operands = (
        span_states, kv_weight, q_weight, q_scale.reshape(group, hd), out_weight,
        decode_states.reshape(nrow, depth), prior_keys.reshape(prior, hd), prior_values.reshape(prior, hd),
        key_scale.reshape(1, hd),
    )
    out, kv = pl.pallas_call(
        functools.partial(kernel, nz, nh),
        out_shape=(
            jax.ShapeDtypeStruct((steps, seqs // nh, ocols), BF16),
            jax.ShapeDtypeStruct((2, nz * pos, hd), BF16),
        ),
        in_specs=[pl.BlockSpec(memory_space=pl.ANY)] * 10,
        out_specs=(vspec,) * 2,
        scratch_shapes=[
            *[vm(a.shape, a.dtype) for a in operands], pltpu.SMEM((1,), jnp.int32), dma((len(operands) + 1,)),
            vm((G, G, blk, feats), BF16),
            vm((hpg, feats, 2 * hd), BF16),
            vm((nh, 2, G * blk, hd), BF16),
            vm((nh, 2, G * blk, hd), BF16),
            vm((2, nz, pos, hd), BF16),
            vm((2, nz, pos, hd), BF16),
            vm((2, nrow // 2, width), F32),
            vm((nrow // 2, width), F32),
            vm((nrow // 4, width), F32),
            vm((nrow // 4, 1, width), F32),
            vm((up_n, steps, 1, width), F32),
            vm((dn_n, steps, 1, width), F32),
            vm((steps * group, hd), F32),
            vm((16, hd), F32),
            vm((16, hd), F32),
            vm((nz, G, steps * group, hd), BF16),
            vm((seqs * steps * group, hd), F32),
            vm((nrow, qcols), BF16),
            vm((steps, seqs, ocols), F32),
            vm((nh, steps, seqs // nh, ocols), F32),
            dma((hpg,)), dma((hpg,)), dma((hpg * CUTS, nz)), dma((up_n, hpg * CUTS)), dma((up_n, hpg * CUTS)),
            dma, dma, dma((G,)), dma((G,)), dma((G,)), dma((G,)),
            dma, dma, dma, dma, dma((up_n,)), dma((up_n,)), dma((dn_n,)), dma((dn_n,)),
            dma((nh, 2)), dma((nh, 2)), dma((2, nz)), dma((2, nz)), dma((nz,)), dma((nz,)),
            dma((nz,)), dma((nz,)), dma((2, nz)), dma((2, nz)), dma((nh,)), dma((nh,)),
        ],
        compiler_params=pltpu.CompilerParams(
            collective_id=0, has_side_effects=True, vmem_limit_bytes=60 * 2**20
        ),
        name="layer",
    )(*operands, cached_len)
    return pl.pallas_call(
        place,
        out_shape=(
            jax.ShapeDtypeStruct(out.shape, BF16),
            jax.ShapeDtypeStruct((1, nz * pos, hd), BF16),
            jax.ShapeDtypeStruct((1, nz * pos, hd), BF16),
        ),
        in_specs=[pl.BlockSpec(memory_space=pl.ANY)] * 2,
        out_specs=(pl.BlockSpec(memory_space=pl.ANY),) * 3,
        scratch_shapes=[dma((3,))],
        compiler_params=pltpu.CompilerParams(vmem_limit_bytes=60 * 2**20),
        name="place",
    )(out, kv)


def solution(mesh):
    return jax.shard_map(
        body,
        mesh=mesh,
        in_specs=(
            P("ctx", None, "head"),
            P("ctx", "head"),
            P("ctx", "head"),
            P("head"),
            P("head", "ctx"),
            P(None, None, "ctx"),
            P("ctx", None, "head"),
            P("ctx", None, "head"),
            P("head"),
            P("ctx"),
        ),
        out_specs=(P(None, "head", "ctx"), P("ctx", None, "head"), P("ctx", None, "head")),
        check_vma=False,
    )
```

```python
import functools

import jax
import jax.numpy as jnp
from jax import lax
from jax.experimental import pallas as pl
from jax.experimental.pallas import tpu as pltpu
from jax.sharding import PartitionSpec as P

MESH = pl.DeviceIdType.MESH
G = 4
CUTS = 2
F32 = jnp.float32
BF16 = jnp.bfloat16


def onehot(rows, cols, source):
    r = lax.broadcasted_iota(jnp.int32, (rows, cols), 0)
    k = lax.broadcasted_iota(jnp.int32, (rows, cols), 1)
    return jnp.where(k == source(r), 1.0, 0.0).astype(BF16)


def dot(a, b):
    return jnp.dot(a, b, preferred_element_type=F32)


def dot_t(a, b):
    return lax.dot_general(a, b, (((1,), (1,)), ((), ())), preferred_element_type=F32)


def kernel(
    nz, nh,
    span_hbm, kvw_hbm, qw_hbm, qs_hbm, ow_hbm, dec_hbm, pk_hbm, pv_hbm, ks_hbm, cl_hbm,
    out_ref, kv_ref,
    span_ref, kvw_ref, qw_ref, qs_ref, ow_ref, dec_ref, pk_ref, pv_ref, ks_ref, cl_ref, in_s,
    spanbuf, wbuf, part, rsbuf, a2abuf, kvnew,
    qbuf, qrecv1, qrecv2, qrow, qup, qdn, qsc, fk, fv,
    gath, gf, lhs, obuf, orecv,
    perm_s, perm_r, w_r, up_s, dn_s,
    spc_s, spc_r, spy_s, spy_r, spf_s, spf_r,
    q1_s, q1_r, q2_s, q2_r, qu_s, qu_r, qd_s, qd_r,
    rs_s, rs_r, a2_s, a2_r, ga_s, ga_r, gy_s, gy_r, gc_s, gc_r, or_s, or_r,
):
    hpg = nh // G
    up_n, dn_n = nz // 2, nz // 2 - 1
    positions, seqs, feats = span_ref.shape
    hd = ks_ref.shape[1]
    group = qs_ref.shape[0]
    steps = dec_ref.shape[0] // seqs
    qcols = group * hd
    blk = positions * nz
    crows = kvw_ref.shape[0] // hpg
    c, h = lax.axis_index("ctx"), lax.axis_index("head")
    z, g = c // G, c % G
    yl, co = g // 2, g % 2
    core_dev = (z * G + yl * 2 + (1 - co), h)
    y_dev = (z * G + (1 - yl) * 2 + co, h)
    up_dev = (lax.rem(z + 1, nz) * G + g, h)
    dn_dev = (lax.rem(z + nz - 1, nz) * G + g, h)

    def zmod(a):
        return lax.rem(a + 2 * nz, nz)

    def rc(src, dst, ss, rs, dev):
        return pltpu.make_async_remote_copy(
            src_ref=src, dst_ref=dst, send_sem=ss, recv_sem=rs, device_id=dev, device_id_type=MESH
        )

    def other(dev):
        return jnp.logical_or(dev[0] != c, dev[1] != h)

    def group_of(head):
        pair = head // hpg
        return (pair // 2 + pair % 2) % 2 * 2 + pair % 2

    def heads_of(p):
        return ((co + yl) % 2 * 2 + co) * hpg + p

    per = (G * nz) // nh

    def perm_to(r):
        v = yl + 2 * co
        j = v if r == 0 else nz // 2 - 1 - v
        zeta = jnp.where(lax.rem(c, per) >= G, zmod(z + j), zmod(z - j))
        return (zeta * G + group_of(h), c // per)

    def slot_of(zeta):
        away = zmod(zeta - h * per // G)
        upper = jnp.logical_and(away >= 1, away <= nz // 2)
        j = jnp.where(upper, away - 1, lax.rem(nz - away, nz))
        r = jnp.where(j >= G, 1, 0)
        v = jnp.where(j >= G, nz // 2 - 1 - j, j)
        cl = jnp.where(upper, G, 0) + lax.rem(v, 2) * 2 + v // 2
        return cl, r

    def perm_from(p):
        cl, _ = slot_of(z)
        return (h * per + cl, heads_of(p))

    def rs_to(d):
        return (z * G + d % G, heads_of(d // G))

    def rs_from(hs):
        return (z * G + group_of(h), hs)

    pending = []

    def finish():
        for leave in pending:
            leave()

    def sent(*copies):
        pending.extend(copy.wait_send for copy in copies)

    fetches = [
        pltpu.make_async_copy(src, dst, in_s.at[i])
        for i, (src, dst) in enumerate((
            (dec_hbm, dec_ref), (qw_hbm, qw_ref), (kvw_hbm, kvw_ref), (span_hbm, span_ref), (ks_hbm, ks_ref),
            (qs_hbm, qs_ref), (pk_hbm, pk_ref), (pv_hbm, pv_ref), (ow_hbm, ow_ref), (cl_hbm, cl_ref),
        ))
    ]
    for fetch in fetches:
        fetch.start()

    barrier = pltpu.get_barrier_semaphore()

    def greet(dev):
        pl.semaphore_signal(barrier, inc=1, device_id=dev, device_id_type=MESH)

    greet(core_dev)
    greet(y_dev)

    def greet_z(i, _):
        greet((zmod(z + i) * G + g, h))
        return 0

    def greet_h(i, _):
        greet((c, lax.rem(h + i, nh)))
        return 0

    lax.fori_loop(1, nz, greet_z, 0)
    lax.fori_loop(1, nh, greet_h, 0)
    for p in range(hpg):
        dev = perm_from(p)

        @pl.when(other(dev))
        def _():
            greet(dev)

    def greet_rs(hs, _):
        dev = rs_from(hs)

        @pl.when(other(dev))
        def _():
            greet(dev)

        return 0

    lax.fori_loop(0, nh, greet_rs, 0)

    peers = 2 + (nz - 1) + (nh - 1)
    for r in range(hpg):
        peers = peers + jnp.where(other(perm_to(r)), 1, 0)
    for d in range(nh):
        peers = peers + jnp.where(other(rs_to(d)), 1, 0)
    pl.semaphore_wait(barrier, peers)

    def wrows(p, slot):
        return wbuf.at[p, pl.ds(pl.multiple_of(slot * crows, crows), crows), :]

    prows = crows // CUTS

    def wslot(m, zeta):
        cl, r = slot_of(zeta)
        start = (cl * hpg + r) * crows + (m % CUTS) * prows
        return wbuf.at[m // CUTS, pl.ds(pl.multiple_of(start, prows), prows), :]

    def perm_copy(r):
        dev = perm_to(r)
        p = h % hpg
        slot = lax.rem(c, per) * hpg + r
        return rc(kvw_hbm.at[pl.ds(r * crows, crows), :], wrows(p, slot), perm_s.at[r], perm_r.at[p], dev), dev

    for r in range(hpg):
        copy, dev = perm_copy(r)

        @pl.when(other(dev))
        def _():
            copy.start()

        @pl.when(jnp.logical_not(other(dev)))
        def _():
            here = wrows(h % hpg, lax.rem(c, per) * hpg + r)
            own_block = pltpu.make_async_copy(kvw_hbm.at[pl.ds(r * crows, crows), :], here, perm_s.at[r])
            own_block.start()
            own_block.wait()

    for r in range(hpg):
        def leave(r=r):
            copy, dev = perm_copy(r)
            pl.when(other(dev))(copy.wait_send)

        pending.append(leave)

    for i in range(4):
        fetches[i].wait()
    order = onehot(seqs, seqs, lambda r: (r % nz) * G + r // nz)
    for p in range(positions):
        rows = dot(order, span_ref[p]).astype(BF16)
        for k in range(G):
            spanbuf[k, g, p * nz:(p + 1) * nz, :] = rows[k * nz:(k + 1) * nz]

    nrow = steps * seqs
    pick = onehot(
        nrow, nrow,
        lambda r: (r % steps) * seqs
        + ((r // steps) % nz) * G + ((r // (steps * nz)) % 2) * 2 + r // (steps * nz * 2),
    )
    decp = dot(pick, dec_ref[...]).astype(BF16)
    half = nrow // 2
    for k in range(2):
        qbuf[k, :, 0:qcols] = dot(decp[k * half:(k + 1) * half], qw_ref[...])
        qbuf[k, :, qcols:] = dot(decp[k * half:(k + 1) * half], kvw_ref[...])

    q1 = rc(qbuf.at[1 - co], qrecv1, q1_s, q1_r, core_dev)
    q1.start()
    spc = rc(spanbuf.at[:, g], spanbuf.at[:, g], spc_s, spc_r, core_dev)
    spc.start()
    q1.wait_recv()
    qh = half // 2
    for k in range(2):
        qbuf[co, k * qh:(k + 1) * qh, :] = qbuf[co, k * qh:(k + 1) * qh, :] + qrecv1[k * qh:(k + 1) * qh, :]
    q2 = rc(qbuf.at[co, pl.ds(pl.multiple_of((1 - yl) * qh, qh), qh), :], qrecv2, q2_s, q2_r, y_dev)
    q2.start()

    def spy(k):
        return rc(spanbuf.at[k, g], spanbuf.at[k, g], spy_s.at[k], spy_r.at[k], y_dev)

    def spf(k):
        gy = (1 - yl) * 2 + co
        return rc(spanbuf.at[k, gy], spanbuf.at[k, gy], spf_s.at[k], spf_r.at[k], core_dev)

    for k in range(G):
        spy(k).start()
    sent(q1, q2, spc, *[spy(k) for k in range(G)])

    def recv_w(m, zeta):
        rc(wslot(m, zeta), wslot(m, zeta), up_s.at[0, 0], w_r.at[m, zeta], up_dev).wait_recv()

    def send_up(s, m):
        zeta = zmod(z - s)
        return rc(wslot(m, zeta), wslot(m, zeta), up_s.at[s, m], w_r.at[m, zeta], up_dev)

    def send_dn(s, m):
        zeta = zmod(z + s)
        return rc(wslot(m, zeta), wslot(m, zeta), dn_s.at[s, m], w_r.at[m, zeta], dn_dev)

    def qpart(d):
        return qrow.at[pl.ds(d * steps, steps)]

    for p in range(hpg):
        cl, r = slot_of(z)
        block = wrows(p, cl * hpg + r)
        pl.when(other(perm_from(p)))(rc(block, block, perm_s.at[0], perm_r.at[p], up_dev).wait_recv)
        for m in range(p * CUTS, (p + 1) * CUTS):
            send_up(0, m).start()
            send_dn(0, m).start()

    def q_up(s):
        src = qpart(zmod(z + up_n)) if s == 0 else qup.at[s - 1]
        return rc(src, qup.at[s], qu_s.at[s], qu_r.at[s], up_dev)

    def q_dn(s):
        src = qpart(zmod(z - dn_n)) if s == 0 else qdn.at[s - 1]
        return rc(src, qdn.at[s], qd_s.at[s], qd_r.at[s], dn_dev)

    def q_step(s):
        if s == 0:
            q2.wait_recv()
            own = qbuf[co, pl.ds(pl.multiple_of(yl * qh, qh), qh), :] + qrecv2[...]
            for r in range(qh):
                qrow[r, 0:1, :] = own[r:r + 1, :]
        else:
            q_up(s - 1).wait_recv()
            qup[s - 1] = qup[s - 1] + qpart(zmod(z + up_n - s))[...]
        q_up(s).start()
        if s < dn_n:
            if s > 0:
                q_dn(s - 1).wait_recv()
                qdn[s - 1] = qdn[s - 1] + qpart(zmod(z - dn_n + s))[...]
            q_dn(s).start()

    parts = hpg * CUTS

    def goes_up(s, m):
        return s < up_n - 1 or m < parts // 2

    def goes_dn(s, m):
        return s < up_n - 1 or m >= parts // 2

    for s in range(1, up_n):
        for m in range(parts):
            recv_w(m, zmod(z - s))
            if goes_up(s, m):
                send_up(s, m).start()
            recv_w(m, zmod(z + s))
            if goes_dn(s, m):
                send_dn(s, m).start()
            if m == parts // 2 - 1 and s >= 2:
                q_step(s - 2)
        k = s - up_n + G
        if k >= 0:
            spy(k).wait_recv()
            spf(k).start()
    q_step(up_n - 2)
    for m in range(parts):
        recv_w(m, zmod(z - up_n))
    spc.wait_recv()
    for k in range(G):
        spf(k).wait_recv()

    sent(*[spf(k) for k in range(G)])
    for s in range(up_n):
        sent(*[send_up(s, m) for m in range(parts) if goes_up(s, m)], q_up(s))
        sent(*[send_dn(s, m) for m in range(parts) if goes_dn(s, m)])
        if s < dn_n:
            sent(q_dn(s))

    def rs_copy(d, kind):
        return rc(part.at[d, kind], rsbuf.at[h, kind], rs_s.at[d, kind], rs_r.at[h, kind], rs_to(d))

    def product(i, _):
        d = lax.rem(i + h, nh)
        tile = spanbuf[d % G].reshape(G * blk, feats)
        sums = dot(tile, wbuf[d // G]).astype(BF16)
        part[d, 0] = sums[:, :hd]
        part[d, 1] = sums[:, hd:]
        away = other(rs_to(d))

        @pl.when(away)
        def _():
            rs_copy(d, 0).start()

        @pl.when(jnp.logical_not(away))
        def _():
            rsbuf[h] = part[d]

        return 0

    lax.fori_loop(0, nh, product, 0)

    def send_values(i, _):
        d = lax.rem(i + h, nh)
        pl.when(other(rs_to(d)))(lambda: rs_copy(d, 1).start())
        return 0

    lax.fori_loop(0, nh, send_values, 0)

    def rs_done(d, _):
        @pl.when(other(rs_to(d)))
        def _():
            rs_copy(d, 0).wait_send()
            rs_copy(d, 1).wait_send()

        return 0

    pending.append(lambda: lax.fori_loop(0, nh, rs_done, 0))

    q_step(up_n - 1)
    q_up(up_n - 1).wait_recv()
    q_dn(dn_n - 1).wait_recv()
    qv = qpart(z)[...] + qup[up_n - 1] + qdn[dn_n - 1]
    for i in range(4, len(fetches)):
        fetches[i].wait()
    ks = ks_ref[...]
    fk[...] = jnp.zeros_like(fk)
    fv[...] = jnp.zeros_like(fv)
    for t in range(steps):
        for j in range(group):
            qsc[t * group + j:t * group + j + 1, :] = qv[t, 0:1, j * hd:(j + 1) * hd]
        fk[t:t + 1, :] = qv[t, 0:1, qcols:qcols + hd] / ks
        fv[t:t + 1, :] = qv[t, 0:1, qcols + hd:qcols + 2 * hd]
    scale = jnp.concatenate([qs_ref[...]] * steps, 0)
    scaled = (qsc[...] * scale * ks * (hd ** -0.5)).astype(BF16)
    s_old = dot_t(scaled, pk_ref[...])
    where = lax.broadcasted_iota(jnp.int32, s_old.shape, 1)
    s_old = jnp.where(where < cl_ref[0], s_old, -1e30)
    s_fresh = dot_t(scaled, fk[...].astype(BF16))
    col = lax.broadcasted_iota(jnp.int32, s_fresh.shape, 1)
    row = lax.broadcasted_iota(jnp.int32, s_fresh.shape, 0)
    s_fresh = jnp.where(col <= row // group, s_fresh, -1e30)
    top0 = jnp.maximum(jnp.max(s_old, 1, keepdims=True), jnp.max(s_fresh, 1, keepdims=True))

    pos = G * positions
    spread = onehot(G * blk, G * blk, lambda r: (r % pos) * nz + r // pos)

    def slot_at(zr, zs):
        return zmod(zs - (zr - zr % 2) + nz // 2)

    def place_of(zs):
        return slot_at(z, zs)

    def zig(i):
        return zmod(z + jnp.where(lax.rem(i, 2) == 1, (i + 1) // 2, -(i // 2)))

    def a2_copy(i, kind):
        zt = zig(nz - i)
        return rc(a2abuf.at[kind, zt], kvnew.at[kind, z], a2_s.at[kind, i], a2_r.at[kind, z], (zt * G + g, h))

    def a2_done(i, _):
        a2_copy(i, 0).wait_send()
        a2_copy(i, 1).wait_send()
        return 0

    for kind in range(2):
        for hs in range(nh):
            slot = rsbuf.at[hs, kind]
            pl.when(other(rs_from(hs)))(rc(slot, slot, rs_s.at[0, 0], rs_r.at[hs, kind], core_dev).wait_recv)
        sums = rsbuf[0, kind].astype(F32)
        for hs in range(1, nh):
            sums = sums + rsbuf[hs, kind].astype(F32)
        if kind == 0:
            sums = sums / ks
        a2abuf[kind] = dot(spread, sums.astype(BF16)).astype(BF16).reshape(nz, pos, hd)

        def a2_start(i, _, kind=kind):
            a2_copy(i, kind).start()
            return 0

        lax.fori_loop(1, nz, a2_start, 0)
        kvnew[kind, z] = a2abuf[kind, z]

    pending.append(lambda: lax.fori_loop(1, nz, a2_done, 0))

    def arrived(kind):
        def a2_wait(i, _):
            zt = zig(i)
            slot = kvnew.at[kind, zt]
            rc(slot, slot, a2_s.at[0, 0], a2_r.at[kind, zt], core_dev).wait_recv()
            return 0

        lax.fori_loop(1, nz, a2_wait, 0)
        return kvnew[kind].reshape(nz * pos, hd)

    k_new = arrived(0)
    s_new = dot_t(scaled, k_new)
    top = jnp.maximum(top0, jnp.max(s_new, 1, keepdims=True))
    w_old, w_new, w_fresh = jnp.exp(s_old - top), jnp.exp(s_new - top), jnp.exp(s_fresh - top)
    total = (
        jnp.sum(w_old, 1, keepdims=True) + jnp.sum(w_new, 1, keepdims=True) + jnp.sum(w_fresh, 1, keepdims=True)
    )
    mixed = dot(w_old.astype(BF16), pv_ref[...]) + dot(w_fresh.astype(BF16), fv[...].astype(BF16))
    v_new = arrived(1)
    kv_ref[...] = kvnew[...].reshape(kv_ref.shape)
    mixed = (mixed + dot(w_new.astype(BF16), v_new)) / total
    gath[place_of(z), g] = mixed.astype(BF16)

    gy_of = (1 - yl) * 2 + co

    def ga_copy(i):
        zt = zig(nz - i)
        return rc(gath.at[place_of(z), g], gath.at[slot_at(zt, z), g], ga_s.at[i], ga_r.at[slot_at(zt, z)], (zt * G + g, h))

    def ga_start(i, _):
        ga_copy(i).start()
        return 0

    lax.fori_loop(1, nz, ga_start, 0)
    batches = ((6, 5), (3, 3), (11, 3), (0, 3), (14, 2)) if nz == 16 else ((0, nz),)

    def gy_copy(b):
        first, count = batches[b]
        ref = gath.at[pl.ds(first, count), g]
        return rc(ref, ref, gy_s.at[b], gy_r.at[b], y_dev)

    def gc_copy(b, k):
        first, count = batches[b]
        ref = gath.at[pl.ds(first, count), g if k == 0 else gy_of]
        return rc(ref, ref, gc_s.at[k, b], gc_r.at[k, b], core_dev)

    for b, (first, count) in enumerate(batches):
        def ga_wait(i, _):
            slot = gath.at[i, g]
            pl.when(i != place_of(z))(rc(slot, slot, ga_s.at[0], ga_r.at[i], core_dev).wait_recv)
            return 0

        lax.fori_loop(first, first + count, ga_wait, 0)
        gy_copy(b).start()
        gc_copy(b, 0).start()
    for b, (first, count) in enumerate(batches):
        slot = gath.at[pl.ds(first, count), gy_of]
        rc(slot, slot, ga_s.at[0], gy_r.at[b], core_dev).wait_recv()
        gc_copy(b, 1).start()
    for b, (first, count) in enumerate(batches):
        for k in range(2):
            slot = gath.at[pl.ds(first, count), (yl if k == 0 else 1 - yl) * 2 + 1 - co]
            rc(slot, slot, ga_s.at[0], gc_r.at[k, b], core_dev).wait_recv()

    def ga_done(i, _):
        ga_copy(i).wait_send()
        return 0

    pending.append(lambda: lax.fori_loop(1, nz, ga_done, 0))
    for b in range(len(batches)):
        sent(gy_copy(b), gc_copy(b, 0), gc_copy(b, 1))

    gf[...] = gath[...].reshape(gf.shape).astype(F32)
    for t in range(steps):
        for j in range(group):
            rows = gf[pl.ds(t * group + j, seqs, stride=steps * group), :]
            lhs[t * seqs:(t + 1) * seqs, j * hd:(j + 1) * hd] = rows.astype(BF16)
    obuf[...] = dot(lhs[...], ow_ref[...]).reshape(obuf.shape)
    mine = seqs // nh

    def rows_of(head):
        return pl.multiple_of(place_of(head * mine // G) * G, mine)

    def or_copy(i):
        ht = lax.rem(h + i, nh)
        src = obuf.at[:, pl.ds(rows_of(ht), mine), :]
        return rc(src, orecv.at[h], or_s.at[i], or_r.at[h], (c, ht))

    def or_start(i, _):
        or_copy(i).start()
        return 0

    lax.fori_loop(1, nh, or_start, 0)
    orecv[h] = obuf[:, pl.ds(rows_of(h), mine), :]

    def or_wait(i, _):
        hs = lax.rem(h + i, nh)
        rc(orecv.at[hs], orecv.at[hs], or_s.at[0], or_r.at[hs], core_dev).wait_recv()
        return 0

    lax.fori_loop(1, nh, or_wait, 0)
    def or_done(i, _):
        or_copy(i).wait_send()
        return 0

    pending.append(lambda: lax.fori_loop(1, nh, or_done, 0))
    result = orecv[0]
    for hs in range(1, nh):
        result = result + orecv[hs]
    out_ref[...] = result.astype(BF16)

    finish()


def place(out_ref, kv_ref, attn_ref, nk_ref, nv_ref):
    attn_ref[...] = out_ref[...]
    nk_ref[0] = kv_ref[0]
    nv_ref[0] = kv_ref[1]


def body(
    span_states, kv_weight, q_weight, q_scale, out_weight, decode_states, prior_keys, prior_values, key_scale, cached_len
):
    nh = lax.axis_size("head")
    nz = lax.axis_size("ctx") // G
    hpg = nh // G
    positions, seqs, feats = span_states.shape
    hd = key_scale.shape[0]
    qcols = q_scale.shape[0]
    group = qcols // hd
    steps, _, depth = decode_states.shape
    width = qcols + 2 * hd
    nrow = steps * seqs
    blk = positions * nz
    pos = G * positions
    ocols = out_weight.shape[1]
    prior = prior_keys.shape[1]
    vm = pltpu.VMEM
    dma = pltpu.SemaphoreType.DMA
    up_n, dn_n = nz // 2, nz // 2 - 1
    vspec = pl.BlockSpec(memory_space=pltpu.VMEM)
    operands = (
        span_states, kv_weight, q_weight, q_scale.reshape(group, hd), out_weight,
        decode_states.reshape(nrow, depth), prior_keys.reshape(prior, hd), prior_values.reshape(prior, hd),
        key_scale.reshape(1, hd),
    )
    out, kv = pl.pallas_call(
        functools.partial(kernel, nz, nh),
        out_shape=(
            jax.ShapeDtypeStruct((steps, seqs // nh, ocols), BF16),
            jax.ShapeDtypeStruct((2, nz * pos, hd), BF16),
        ),
        in_specs=[pl.BlockSpec(memory_space=pl.ANY)] * 10,
        out_specs=(vspec,) * 2,
        scratch_shapes=[
            *[vm(a.shape, a.dtype) for a in operands], pltpu.SMEM((1,), jnp.int32), dma((len(operands) + 1,)),
            vm((G, G, blk, feats), BF16),
            vm((hpg, feats, 2 * hd), BF16),
            vm((nh, 2, G * blk, hd), BF16),
            vm((nh, 2, G * blk, hd), BF16),
            vm((2, nz, pos, hd), BF16),
            vm((2, nz, pos, hd), BF16),
            vm((2, nrow // 2, width), F32),
            vm((nrow // 2, width), F32),
            vm((nrow // 4, width), F32),
            vm((nrow // 4, 1, width), F32),
            vm((up_n, steps, 1, width), F32),
            vm((dn_n, steps, 1, width), F32),
            vm((steps * group, hd), F32),
            vm((16, hd), F32),
            vm((16, hd), F32),
            vm((nz, G, steps * group, hd), BF16),
            vm((seqs * steps * group, hd), F32),
            vm((nrow, qcols), BF16),
            vm((steps, seqs, ocols), F32),
            vm((nh, steps, seqs // nh, ocols), F32),
            dma((hpg,)), dma((hpg,)), dma((hpg * CUTS, nz)), dma((up_n, hpg * CUTS)), dma((up_n, hpg * CUTS)),
            dma, dma, dma((G,)), dma((G,)), dma((G,)), dma((G,)),
            dma, dma, dma, dma, dma((up_n,)), dma((up_n,)), dma((dn_n,)), dma((dn_n,)),
            dma((nh, 2)), dma((nh, 2)), dma((2, nz)), dma((2, nz)), dma((nz,)), dma((nz,)),
            dma((5,)), dma((5,)), dma((2, 5)), dma((2, 5)), dma((nh,)), dma((nh,)),
        ],
        compiler_params=pltpu.CompilerParams(
            collective_id=0, has_side_effects=True, vmem_limit_bytes=60 * 2**20
        ),
        name="layer",
    )(*operands, cached_len)
    return pl.pallas_call(
        place,
        out_shape=(
            jax.ShapeDtypeStruct(out.shape, BF16),
            jax.ShapeDtypeStruct((1, nz * pos, hd), BF16),
            jax.ShapeDtypeStruct((1, nz * pos, hd), BF16),
        ),
        in_specs=[vspec] * 2,
        out_specs=(vspec,) * 3,
        name="place",
    )(out, kv)


def solution(mesh):
    return jax.shard_map(
        body,
        mesh=mesh,
        in_specs=(
            P("ctx", None, "head"),
            P("ctx", "head"),
            P("ctx", "head"),
            P("head"),
            P("head", "ctx"),
            P(None, None, "ctx"),
            P("ctx", None, "head"),
            P("ctx", None, "head"),
            P("head"),
            P("ctx"),
        ),
        out_specs=(P(None, "head", "ctx"), P("ctx", None, "head"), P("ctx", None, "head")),
        check_vma=False,
    )
```
